256 devices in a mesh: dp: 4 (over y), tensor: 4 (over x), latent: 16 (over z, core).
Axes of the slice: x: 4, y: 4, z: 8, core: 2. Of those that a mesh axis runs over, the one named last changes fastest.
Arguments:
- resid: bfloat16 [1024, 3584], P('dp', ('tensor', 'latent')), may hold values from -6 to 6
- out_grad: bfloat16 [1024, 3584], P('dp', ('tensor', 'latent')), may hold values from -6 to 6
- norm_gain: float32 [3584], replicated, may hold values from 0.25 to 1.75
- w_gate: bfloat16 [3584, 14336], P('dp', ('tensor', 'latent')), may hold values from -0.09375 to 0.09375
- w_up: bfloat16 [3584, 14336], P('dp', ('tensor', 'latent')), may hold values from -0.09375 to 0.09375
- w_down_t: bfloat16 [3584, 14336], P('dp', ('tensor', 'latent')), may hold values from -0.046875 to 0.046875
- decoder: bfloat16 [65536, 3584], P('latent', 'tensor'), may hold values from -0.09375 to 0.09375
- dec_bias: float32 [3584], replicated, may hold values from -5 to 5
- block_ids: int32 [8, 32], P('dp'), may hold values from 0 to 511, as said below
- counts: int32 [8], P('dp'), may hold values from 1 to 32, as said below
- latent_acts: bfloat16 [1024, 4096], P(('dp', 'tensor', 'latent')), may hold values from 0.099609375 to 4
Outputs:
- scores: bfloat16 [1024, 4096], P(('dp', 'tensor', 'latent'))
- error_score: float32 [1024], P(('dp', 'tensor', 'latent'))
The draws below stay inside these ranges and needn't reach their ends.
Inputs may be any that keep to these rules, and one draw needn't show every extreme that they name: `block_ids`: within a row the ids are distinct; no latent index (id // 32) owns more than 8 of a row's 32 ids, and in every row one owns exactly 8. Slots k < counts[b] are live; 32 is reached in some row of every draw.
All inputs are finite; a program needn't handle non-finite values.
Results may differ from the reference program's by a relative error of at most 0.017.
Values may be sent and summed in bfloat16 or wider, within the bound.
No kernel may reach another device: no remote copies, remote signals or barrier semaphores. Data moves between devices by JAX's collectives and lax.ppermute only.
A program may use at most 64 MiB of HBM per device.

```python
import math
import jax
import jax.numpy as jnp
from jax import lax

D = 3584
FF = 14336
TOKEN_BLOCK = 128
LATENT_BLOCK = 128
BLOCKS_DEV = 32
ACTIVE = 32
CAPACITY = 8
LATENTS = 65536
TOKENS = 1024
TOKEN_BLOCKS = 8
N_LATENT = 16


def shuffled(subkey, length):
    return jax.random.permutation(subkey, length)


def draw_block_ids(key, part):
    key = jax.random.fold_in(key, 11)
    hot_key, local_key, order_key = jax.random.split(key, 3)
    hot_owner = jax.random.randint(hot_key, (TOKEN_BLOCKS, 1), 0, N_LATENT)
    slot_index = jnp.arange(ACTIVE, dtype=jnp.int32)
    offset = jnp.where(slot_index < CAPACITY, 0, (slot_index - CAPACITY) % max(N_LATENT - 1, 1) + 1)
    owners = (hot_owner + offset[None, :]) % N_LATENT
    local_perm = jax.vmap(lambda subkey: shuffled(subkey, BLOCKS_DEV))(jax.random.split(local_key, TOKEN_BLOCKS))[:, :ACTIVE]
    block_numbers = owners * BLOCKS_DEV + local_perm
    order = jax.vmap(lambda subkey: shuffled(subkey, ACTIVE))(jax.random.split(order_key, TOKEN_BLOCKS))
    return jnp.take_along_axis(block_numbers, order, axis=1).astype(jnp.int32)


def draw_counts(key, part):
    key = jax.random.fold_in(key, 12)
    count_key, row_key = jax.random.split(key)
    drawn = jax.random.randint(count_key, (TOKEN_BLOCKS,), 1, ACTIVE + 1)
    full_row = jax.random.randint(row_key, (), 0, TOKEN_BLOCKS)
    return jnp.where(jnp.arange(TOKEN_BLOCKS) == full_row, ACTIVE, drawn).astype(jnp.int32)


def steps_of(key, shape, pieces, least, top_value):
    def one(position, shards_of):
        steps = jax.random.uniform(jax.random.fold_in(jax.random.fold_in(key, 6), position), (shards_of,), jnp.float32, least / len(pieces), top_value / len(pieces))
        return jnp.repeat(jnp.exp(steps), shape[position] // shards_of).reshape((-1,) + (1,) * (len(shape) - position - 1))

    gain = one(*pieces[0])
    for cut in pieces[1:]:
        gain = gain * one(*cut)
    return gain


def normal_values(own_key, extent, width, bound, shards=(), kind=jnp.bfloat16):
    level = steps_of(own_key, extent, shards, -0.22, 0.18) if shards else 1.0
    array = jax.random.normal(own_key, extent, jnp.float32) * width * level
    return jnp.minimum(jnp.maximum(array, -bound), bound).astype(kind)


def setup_inputs(seed: int = 0) -> dict:
    arg_keys = jax.random.split(jax.random.key(seed), 12)
    return {
        "resid": normal_values(arg_keys[0], (TOKENS, D), 1.0, 6.0, ((0, 4), (1, 64))),
        "out_grad": normal_values(arg_keys[1], (TOKENS, D), 1.0, 6.0, ((0, 4), (1, 64))),
        "norm_gain": jnp.clip(1.0 + 0.15 * jax.random.normal(arg_keys[2], (D,), jnp.float32), 0.25, 1.75),
        "w_gate": normal_values(arg_keys[3], (D, FF), D ** -0.5, 0.09375, ((0, 4), (1, 64))),
        "w_up": normal_values(arg_keys[4], (D, FF), D ** -0.5, 0.09375, ((0, 4), (1, 64))),
        "w_down_t": normal_values(arg_keys[5], (D, FF), FF ** -0.5, 0.046875, ((0, 4), (1, 64))),
        "decoder": normal_values(arg_keys[6], (LATENTS, D), D ** -0.5, 0.09375, ((0, 16), (1, 4))),
        "dec_bias": normal_values(arg_keys[7], (D,), 1.0, 5.0, (), jnp.float32),
        "block_ids": draw_block_ids(jax.random.fold_in(arg_keys[11], 71), 0),
        "counts": draw_counts(jax.random.fold_in(arg_keys[11], 71), 0),
        "latent_acts": jnp.clip(jnp.exp(math.log(4.0) - 3.6927934 * jax.random.uniform(arg_keys[10], (TOKENS, ACTIVE * LATENT_BLOCK), jnp.float32) ** steps_of(arg_keys[10], (TOKENS, ACTIVE * LATENT_BLOCK), ((0, 256),), -0.2, 0.2)), 0.099609375, 4.0).astype(jnp.bfloat16),
    }


def gelu_parts(gate):
    coeff = math.sqrt(2.0 / math.pi)
    inner = coeff * (gate + 0.044715 * gate * gate * gate)
    hyper = jnp.tanh(inner)
    act = 0.5 * gate * (1.0 + hyper)
    slope = 0.5 * (1.0 + hyper) + 0.5 * gate * (1.0 - hyper * hyper) * coeff * (1.0 + 3.0 * 0.044715 * gate * gate)
    return (act, slope)

def reference(resid, out_grad, norm_gain, w_gate, w_up, w_down_t, decoder, dec_bias, block_ids, counts, latent_acts):
    x_float = resid.astype(jnp.float32)
    root_mean = jnp.sqrt(lax.optimization_barrier(jnp.mean(x_float * x_float, axis=-1, keepdims=True)) + 1e-06)
    x_hat = x_float / root_mean
    normed = (x_hat * norm_gain).astype(jnp.bfloat16)
    gate = jnp.dot(normed, w_gate, preferred_element_type=jnp.float32)
    up_value = jnp.dot(normed, w_up, preferred_element_type=jnp.float32)
    grad_a = jnp.dot(out_grad, w_down_t, preferred_element_type=jnp.float32)
    act, slope = gelu_parts(gate)
    grad_up = (grad_a * act).astype(jnp.bfloat16)
    grad_gate = (grad_a * up_value * slope).astype(jnp.bfloat16)
    grad_norm = jnp.dot(grad_gate, w_gate.T, preferred_element_type=jnp.float32) + jnp.dot(grad_up, w_up.T, preferred_element_type=jnp.float32)
    grad_scaled = grad_norm * norm_gain
    center = lax.optimization_barrier(jnp.mean(grad_scaled * x_hat, axis=-1, keepdims=True))
    grad_x = out_grad.astype(jnp.float32) + (grad_scaled - x_hat * center) / root_mean
    grad_cast = grad_x.astype(jnp.bfloat16)
    decoder_blocks = decoder.reshape(LATENTS // LATENT_BLOCK, LATENT_BLOCK, D)

    def per_block(inputs):
        grad_rows, ids_row, count_row, acts_rows = inputs
        chosen = decoder_blocks[ids_row].reshape(ACTIVE * LATENT_BLOCK, D)
        products = jnp.dot(grad_rows, chosen.T, preferred_element_type=jnp.float32)
        live_slots = (jnp.arange(ACTIVE, dtype=jnp.int32) < count_row).astype(jnp.float32)
        live_cols = jnp.repeat(live_slots, LATENT_BLOCK)
        return products * acts_rows.astype(jnp.float32) * live_cols[None, :]
    score_full = lax.map(per_block, (grad_cast.reshape(TOKEN_BLOCKS, TOKEN_BLOCK, D), block_ids, counts, latent_acts.reshape(TOKEN_BLOCKS, TOKEN_BLOCK, ACTIVE * LATENT_BLOCK)))
    score_full = score_full.reshape(TOKENS, ACTIVE * LATENT_BLOCK)
    error_score = (lax.optimization_barrier(jnp.sum(grad_x * (x_float - dec_bias), axis=-1)) - lax.optimization_barrier(jnp.sum(score_full, axis=-1))) / math.sqrt(D)
    return (score_full.astype(jnp.bfloat16), error_score)
```

```python
import functools
import math

import jax
import jax.numpy as jnp
from jax import lax
from jax.experimental import pallas as pl
from jax.experimental.pallas import tpu as pltpu
from jax.sharding import PartitionSpec as P

BLOCK = 128
N_DP, N_T, N_L, N_Z = 4, 4, 16, 8
TOK = 256
D = 3584
CHUNK = D // N_T
PIECE = CHUNK // N_L
HID = 224
HALF = CHUNK // 2
CAP = 8
SLOTS = 32
SENT = HALF + 16
COLS = CAP * BLOCK
WIDE = COLS + BLOCK
OWN_TOK = TOK // N_T
EPS = 1e-06
F32, BF16 = jnp.float32, jnp.bfloat16

VMEM = pl.BlockSpec(memory_space=pltpu.VMEM)
SMEM = pl.BlockSpec(memory_space=pltpu.SMEM)
ANY = pl.BlockSpec(memory_space=pl.ANY)


def shape(dims, dtype):
    return jax.ShapeDtypeStruct(dims, dtype)


def call(kernel, name, in_specs, outs, scratch=(), limit=48):
    return pl.pallas_call(
        kernel,
        name=name,
        in_specs=in_specs,
        out_specs=jax.tree.map(lambda _: VMEM, outs),
        out_shape=outs,
        scratch_shapes=list(scratch),
        compiler_params=pltpu.CompilerParams(vmem_limit_bytes=limit * 2**20),
    )


def shift(x, axis, size, by):
    return lax.ppermute(x, axis, [(i, (i + by) % size) for i in range(size)])


def swap_core(x):
    return lax.ppermute(x, "latent", [(i, i ^ 1) for i in range(N_L)])


def split(row):
    high = row.astype(BF16).astype(F32)
    return high, row - high


def rows_of(high, low, count):
    index = lax.broadcasted_iota(jnp.int32, (count, high.shape[1]), 0)
    return jnp.where(index == 0, high, jnp.where(index == 1, low, 0.0))


def mlp_kernel(idx, *refs):
    own, other = refs[0:4], refs[4:8]
    gain = refs[8]
    weights = [refs[9 + 5 * i : 14 + 5 * i] for i in range(3)]
    keep, send, cen_out, root_out = refs[24:28]
    x_scr, g_scr, xn_scr, gb_scr, part, out_scr = refs[28:]
    dp, tensor, z, core = idx[0], idx[1], idx[2], idx[3]
    square = jnp.zeros((PIECE, TOK), F32)
    for pieces, side in ((own, core), (other, 1 - core)):
        for e in range(N_T):
            base = lax.rem(tensor - e + N_T, N_T) * CHUNK + side * PIECE
            for d in range(N_Z):
                at = pl.multiple_of(base + lax.rem(z - d + N_Z, N_Z) * 2 * PIECE, 8)
                x = pieces[e][d, 0].astype(F32)
                square += x * x
                x_scr[pl.ds(at, PIECE), :] = x
                g_scr[pl.ds(at, PIECE), :] = pieces[e][d, 1].astype(F32)
    mean = jnp.sum(square, axis=0, keepdims=True) * (1.0 / D)
    root = jnp.sqrt(mean + EPS)
    root_out[...] = root
    inv = 1.0 / root
    step = 448
    for i in range(D // step):
        at = pl.ds(i * step, step)
        xn_scr[at, :] = (x_scr[at, :] * inv * gain[at, :]).astype(BF16)
        gb_scr[at, :] = g_scr[at, :].astype(BF16)

    chunks = (dp, lax.rem(dp + N_DP - 1, N_DP), lax.rem(dp + 1, N_DP), lax.rem(dp + 2, N_DP))
    places = (
        (chunks[0], 0, CHUNK),
        (chunks[1], 0, CHUNK),
        (chunks[2], 0, CHUNK),
        (chunks[3], 0, HALF),
        (chunks[3], HALF, HALF),
    )
    gate = up = grad_a = jnp.zeros((HID, TOK), F32)
    contract = (((0,), (0,)), ((), ()))
    for j, (chunk, offset, size) in enumerate(places):
        at = pl.ds(pl.multiple_of(chunk * CHUNK + offset, 16), size)
        xn, gb = xn_scr[at, :], gb_scr[at, :]
        gate += lax.dot_general(weights[0][j][...], xn, contract, preferred_element_type=F32)
        up += lax.dot_general(weights[1][j][...], xn, contract, preferred_element_type=F32)
        grad_a += lax.dot_general(weights[2][j][...], gb, contract, preferred_element_type=F32)
    coeff = math.sqrt(2.0 / math.pi)
    cube = 0.044715 * gate * gate
    hyper = jnp.tanh(coeff * (gate + cube * gate))
    half = 0.5 * (1.0 + hyper)
    act = gate * half
    slope = half + 0.5 * gate * (1.0 - hyper * hyper) * coeff * (1.0 + 3.0 * cube)
    grad_up = (grad_a * act).astype(BF16)
    grad_gate = (grad_a * up * slope).astype(BF16)
    center = jnp.sum(
        grad_gate.astype(F32) * gate + grad_up.astype(F32) * up, axis=0, keepdims=True
    )
    cen_out[...] = center
    high, low = split(center)
    out_scr[pl.ds(HALF, 16), :] = rows_of(high, low, 16)
    for k in range(4):
        for j in ((k,) if k < 3 else (3, 4)):
            offset = HALF if j == 4 else 0
            part[pl.ds(offset, weights[0][j].shape[0]), :] = jnp.dot(
                weights[0][j][...], grad_gate, preferred_element_type=F32
            ) + jnp.dot(weights[1][j][...], grad_up, preferred_element_type=F32)
        for s in range(N_Z):
            mine = pl.multiple_of(s * 2 * PIECE + core * PIECE, 8)
            theirs = pl.multiple_of(s * 2 * PIECE + (1 - core) * PIECE, 8)
            keep[chunks[k], pl.ds(s * PIECE, PIECE), :] = part[pl.ds(mine, PIECE), :]
            out_scr[pl.ds(s * PIECE, PIECE), :] = part[pl.ds(theirs, PIECE), :]
        send[chunks[k]] = out_scr[...].astype(BF16)


def core_sum_kernel(idx, keep, got, cen, own, s1, s2, s3, cen_out, scr):
    tensor = idx[1]
    tail = got[0].astype(F32)[HALF:, :]
    center = cen[...] + tail[0:1, :] + tail[1:2, :]
    cen_out[...] = center
    high, low = split(center)
    scr[pl.ds(HALF, 16), :] = rows_of(high, low, 16)
    own[...] = keep[tensor] + got[tensor].astype(F32)[:HALF, :]
    for e, out in ((1, s1), (2, s2), (3, s3)):
        to = lax.rem(tensor + e, N_T)
        scr[pl.ds(0, HALF), :] = keep[to] + got[to].astype(F32)[:HALF, :]
        out[...] = scr[...].astype(BF16)


def tensor_sum_kernel(idx, own, r1, r2, r3, cen, *refs):
    mine, sends, cen_out, scr, row = refs[0], refs[1:8], refs[8], refs[9], refs[10]
    z = idx[2]
    total = own[...]
    center = cen[...]
    for r in (r1, r2, r3):
        v = r[...].astype(F32)
        total = total + v[:HALF, :]
        center = center + v[HALF : HALF + 1, :] + v[HALF + 1 : HALF + 2, :]
    cen_out[...] = center
    scr[...] = total
    high, low = split(center)
    row[pl.ds(PIECE, 8), :] = rows_of(high, low, 8)
    mine[...] = scr[pl.ds(pl.multiple_of(z * PIECE, 8), PIECE), :]
    for d in range(1, N_Z):
        at = pl.multiple_of(lax.rem(z + d, N_Z) * PIECE, 8)
        row[pl.ds(0, PIECE), :] = scr[pl.ds(at, PIECE), :]
        sends[d - 1][...] = row[...].astype(BF16)


def grad_kernel(mine, *refs):
    got, (cen, root, gain, bias, x_ref, g_ref, cast, err) = refs[:7], refs[7:]
    total = mine[...]
    center = cen[...]
    for r in got:
        v = r[...].astype(F32)
        total = total + v[:PIECE, :]
        center = center + v[PIECE : PIECE + 1, :] + v[PIECE + 1 : PIECE + 2, :]
    center = center * (1.0 / D)
    x = x_ref[...].astype(F32)
    inv = 1.0 / root[...]
    grad_x = g_ref[...].astype(F32) + (total * gain[...] - x * inv * center) * inv
    cast[...] = grad_x.astype(BF16)
    err[...] = jnp.sum(grad_x * (x - bias[...]), axis=0, keepdims=True)


def decode_kernel(idx, ids, grad, err, decoder, own, s1, s2, s3, dec, wide, sems):
    tensor = idx[1]
    copies = []
    for b in range(2):
        for r in range(CAP):
            rows = pl.ds(pl.multiple_of(ids[b, r] * BLOCK, BLOCK), BLOCK)
            copy = pltpu.make_async_copy(
                decoder.at[rows], dec.at[b, pl.ds(r * BLOCK, BLOCK)], sems.at[b, r]
            )
            copy.start()
            copies.append(copy)
    tall = jnp.broadcast_to(err[...], (BLOCK, TOK)).T
    high, low = split(tall)
    lane = lax.broadcasted_iota(jnp.int32, (TOK, BLOCK), 1)
    wide[:, COLS:] = jnp.where(lane == 0, high, jnp.where(lane == 1, low, 0.0))
    for b in range(2):
        tokens = grad[:, b * BLOCK : (b + 1) * BLOCK]
        for r in range(CAP):
            copies[b * CAP + r].wait()
        wide[b * BLOCK : (b + 1) * BLOCK, :COLS] = lax.dot_general(
            tokens, dec[b], (((0,), (1,)), ((), ())), preferred_element_type=F32
        )
    own[...] = wide[pl.ds(pl.multiple_of(tensor * OWN_TOK, OWN_TOK), OWN_TOK), :]
    for e, out in ((1, s1), (2, s2), (3, s3)):
        to = lax.rem(tensor + e, N_T)
        rows = pl.ds(pl.multiple_of(to * OWN_TOK, OWN_TOK), OWN_TOK)
        out[...] = wide[rows, :].astype(BF16)


def product_sum_kernel(own, r1, r2, r3, out):
    total = own[...]
    for r in (r1, r2, r3):
        total = total + r[...].astype(F32)
    out[:, :COLS] = total[:, :COLS].astype(BF16)
    high, low = split(total[:, COLS : COLS + 1] + total[:, COLS + 1 : COLS + 2])
    lane = lax.broadcasted_iota(jnp.int32, (OWN_TOK, BLOCK), 1)
    out[:, COLS:] = jnp.where(lane == 0, high, jnp.where(lane == 1, low, 0.0)).astype(BF16)


def score_kernel(slots, got, acts, scores, err, scr):
    scr[...] = got[...].astype(F32)
    total = jnp.zeros((4, BLOCK), F32)
    for k in range(SLOTS):
        at = pl.ds(pl.multiple_of(slots[1, k] * BLOCK, BLOCK), BLOCK)
        live = slots[2, k].astype(F32)
        value = scr[slots[0, k], :, at] * (acts[:, k * BLOCK : (k + 1) * BLOCK].astype(F32) * live)
        total += value
        scores[:, k * BLOCK : (k + 1) * BLOCK] = value.astype(BF16)
    extra = jnp.sum(scr[:, :, COLS:], axis=0)
    err[...] = jnp.sum(extra - total, axis=-1, keepdims=True) * (1.0 / math.sqrt(D))


def on_device(
    resid,
    out_grad,
    norm_gain,
    w_gate,
    w_up,
    w_down_t,
    decoder,
    dec_bias,
    block_ids,
    counts,
    latent_acts,
):
    dp, tensor, latent = (lax.axis_index(a) for a in ("dp", "tensor", "latent"))
    idx = jnp.stack([dp, tensor, latent // 2, latent % 2]).astype(jnp.int32)

    with jax.named_scope("weight_rows"):
        pieces = []
        for w in (w_gate, w_up, w_down_t):
            below = shift(w, "dp", N_DP, 1)
            above = shift(w, "dp", N_DP, -1)
            far_low = shift(below[:HALF], "dp", N_DP, 1)
            far_high = shift(above[HALF:], "dp", N_DP, -1)
            pieces += [w, below, above, far_low, far_high]

    with jax.named_scope("token_features"):
        x_own, g_own = resid.T, out_grad.T
        mine = jnp.stack([x_own, g_own])
        column = jnp.stack([mine] + [shift(mine, "latent", N_L, 2 * d) for d in range(1, N_Z)])
        own = [column] + [shift(column, "tensor", N_T, e) for e in range(1, N_T)]
        other = [swap_core(a) for a in own]

    with jax.named_scope("mlp"):
        keep, send, cen, root = call(
            mlp_kernel,
            "mlp",
            [SMEM] + [VMEM] * 24,
            (
                shape((N_T, HALF, TOK), F32),
                shape((N_T, SENT, TOK), BF16),
                shape((1, TOK), F32),
                shape((1, TOK), F32),
            ),
            [
                pltpu.VMEM((D, TOK), F32),
                pltpu.VMEM((D, TOK), F32),
                pltpu.VMEM((D, TOK), BF16),
                pltpu.VMEM((D, TOK), BF16),
                pltpu.VMEM((CHUNK, TOK), F32),
                pltpu.VMEM((SENT, TOK), F32),
            ],
        )(idx, *own, *other, norm_gain[:, None], *pieces)

    with jax.named_scope("hidden_sums"):
        got = swap_core(send)
        row = shape((1, TOK), F32)
        chunk, s1, s2, s3, cen = call(
            core_sum_kernel,
            "core_sum",
            [SMEM] + [VMEM] * 3,
            (shape((HALF, TOK), F32),) + (shape((SENT, TOK), BF16),) * 3 + (row,),
            [pltpu.VMEM((SENT, TOK), F32)],
        )(idx, keep, got, cen)
        got = [shift(s, "tensor", N_T, e) for e, s in ((1, s1), (2, s2), (3, s3))]
        *sends, cen = call(
            tensor_sum_kernel,
            "tensor_sum",
            [SMEM] + [VMEM] * 5,
            (shape((PIECE, TOK), F32),) + (shape((PIECE + 8, TOK), BF16),) * 7 + (row,),
            [pltpu.VMEM((HALF, TOK), F32), pltpu.VMEM((PIECE + 8, TOK), F32)],
        )(idx, chunk, *got, cen)
        got = [shift(s, "latent", N_L, 2 * (i + 1)) for i, s in enumerate(sends[1:])]
        first = (tensor * N_L + latent) * PIECE
        gain_own = lax.dynamic_slice_in_dim(norm_gain, first, PIECE, 0)[:, None]
        bias_own = lax.dynamic_slice_in_dim(dec_bias, first, PIECE, 0)[:, None]
        cast, err = call(
            grad_kernel, "grad", [VMEM] * 14, (shape((PIECE, TOK), BF16), row)
        )(sends[0], *got, cen, root, gain_own, bias_own, x_own, g_own)

    with jax.named_scope("decode"):
        grads = lax.all_gather(cast, "latent", axis=0, tiled=True)
        owner = block_ids // SLOTS
        same = owner[:, :, None] == owner[:, None, :]
        before = jnp.tril(jnp.ones((SLOTS, SLOTS), bool), -1)
        rank = jnp.sum(same & before, axis=2, dtype=jnp.int32)
        takes = (owner == latent)[:, :, None] & (rank[:, :, None] == jnp.arange(CAP))
        local = jnp.sum(jnp.where(takes, (block_ids % SLOTS)[:, :, None], 0), axis=1)
        token_block = tensor // 2
        live = jnp.arange(SLOTS, dtype=jnp.int32) < counts[token_block]
        slots = jnp.stack([owner[token_block], rank[token_block], live.astype(jnp.int32)])
        own, s1, s2, s3 = call(
            decode_kernel,
            "decode",
            [SMEM, SMEM, VMEM, VMEM, ANY],
            (shape((OWN_TOK, WIDE), F32),) + (shape((OWN_TOK, WIDE), BF16),) * 3,
            [
                pltpu.VMEM((2, COLS, CHUNK), BF16),
                pltpu.VMEM((TOK, WIDE), F32),
                pltpu.SemaphoreType.DMA((2, CAP)),
            ],
        )(idx, local.astype(jnp.int32), grads, err, decoder)
        got = [shift(s, "tensor", N_T, e) for e, s in ((1, s1), (2, s2), (3, s3))]
        total = call(
            product_sum_kernel, "product_sum", [VMEM] * 4, shape((OWN_TOK, WIDE), BF16)
        )(own, *got)

    with jax.named_scope("scores"):
        got = lax.all_to_all(total.reshape(N_L, 4, WIDE), "latent", 0, 0, tiled=True)
        scores, err = call(
            score_kernel,
            "score",
            [SMEM, VMEM, VMEM],
            (shape((4, SLOTS * BLOCK), BF16), shape((4, 1), F32)),
            [pltpu.VMEM((N_L, 4, WIDE), F32)],
        )(slots, got, latent_acts)
    return scores, err.reshape(4)


def solution(mesh):
    return jax.shard_map(
        on_device,
        mesh=mesh,
        in_specs=(
            P("dp", ("tensor", "latent")),
            P("dp", ("tensor", "latent")),
            P(),
            P("dp", ("tensor", "latent")),
            P("dp", ("tensor", "latent")),
            P("dp", ("tensor", "latent")),
            P("latent", "tensor"),
            P(),
            P("dp", None),
            P("dp"),
            P(("dp", "tensor", "latent"), None),
        ),
        out_specs=(P(("dp", "tensor", "latent"), None), P(("dp", "tensor", "latent"))),
        check_vma=False,
    )
```

```python
import functools
import math

import jax
import jax.numpy as jnp
from jax import lax
from jax.experimental import pallas as pl
from jax.experimental.pallas import tpu as pltpu
from jax.sharding import PartitionSpec as P

BLOCK = 128
N_DP, N_T, N_L, N_Z = 4, 4, 16, 8
TOK = 256
D = 3584
CHUNK = D // N_T
PIECE = CHUNK // N_L
HID = 224
HALF = CHUNK // 2
CAP = 8
SLOTS = 32
GROUP = HALF // 2
SENT = GROUP + 16
COLS = CAP * BLOCK
WIDE = COLS + BLOCK
OWN_TOK = TOK // N_T
EPS = 1e-06
F32, BF16 = jnp.float32, jnp.bfloat16

VMEM = pl.BlockSpec(memory_space=pltpu.VMEM)
SMEM = pl.BlockSpec(memory_space=pltpu.SMEM)
ANY = pl.BlockSpec(memory_space=pl.ANY)
HBM = pl.BlockSpec(memory_space=pltpu.HBM)


def shape(dims, dtype):
    return jax.ShapeDtypeStruct(dims, dtype)


def call(kernel, name, in_specs, outs, scratch=(), limit=48):
    return pl.pallas_call(
        kernel,
        name=name,
        in_specs=in_specs,
        out_specs=jax.tree.map(lambda _: VMEM, outs),
        out_shape=outs,
        scratch_shapes=list(scratch),
        compiler_params=pltpu.CompilerParams(vmem_limit_bytes=limit * 2**20),
    )


def shift(x, axis, size, by):
    return lax.ppermute(x, axis, [(i, (i + by) % size) for i in range(size)])


def swap_core(x):
    return lax.ppermute(x, "latent", [(i, i ^ 1) for i in range(N_L)])


def split(row):
    high = row.astype(BF16).astype(F32)
    return high, row - high


def rows_of(high, low, count):
    index = lax.broadcasted_iota(jnp.int32, (count, high.shape[1]), 0)
    return jnp.where(index == 0, high, jnp.where(index == 1, low, 0.0))


def mlp_kernel(idx, x0, g0, a1, a2, a3, b1, b2, b3, gain, w0, w1, w2, w3, w4, *refs):
    keep1, keep2, send1, send2, cen_out, root_out = refs[:6]
    x_scr, g_scr, grads, part, out_scr = refs[6:]
    dp, tensor, odd, core = idx[0], idx[1], lax.rem(idx[2], 2), idx[3]
    first = core == 0
    square = jnp.zeros((8, TOK), F32)
    for e, (a, b) in enumerate(((x0, g0), (a1, b1), (a2, b2), (a3, b3))):
        at = pl.ds(pl.multiple_of(lax.rem(tensor - e + N_T, N_T) * CHUNK, 16), CHUNK)
        va, vb = a[...], b[...]
        if e:
            va, vb = jnp.where(first, va, vb), jnp.where(first, vb, va)
        x_scr[at, :] = va
        g_scr[at, :] = vb
        x = va.astype(F32)
        square += jnp.sum((x * x).reshape(CHUNK // 8, 8, TOK), axis=0)
    mean = jnp.sum(square, axis=0, keepdims=True) * (1.0 / D)
    root = jnp.sqrt(mean + EPS)
    root_out[...] = root
    inv = 1.0 / root
    columns = gain[...].T
    for i in range(D // BLOCK):
        at = pl.ds(i * BLOCK, BLOCK)
        x_scr[at, :] = (x_scr[at, :].astype(F32) * inv * columns[:, i : i + 1]).astype(BF16)

    chunks = (dp, lax.rem(dp + N_DP - 1, N_DP), lax.rem(dp + 1, N_DP), lax.rem(dp + 2, N_DP))

    def forward(w, chunk):
        rows = w.shape[1]
        at = pl.ds(pl.multiple_of(chunk * CHUNK, 16), CHUNK)
        both = jnp.dot(
            w[0:2].reshape(2 * rows, CHUNK), x_scr[at, :], preferred_element_type=F32
        )
        down = jnp.dot(w[2], g_scr[at, :], preferred_element_type=F32)
        return both[:rows], both[rows:], down

    low, high = forward(w3, chunks[3]), forward(w4, chunks[3])
    sums = [jnp.concatenate(pair, axis=0) for pair in zip(low, high)]
    for w, chunk in ((w0, chunks[0]), (w1, chunks[1]), (w2, chunks[2])):
        sums = [total + v for total, v in zip(sums, forward(w, chunk))]
    gate, up, grad_a = sums
    coeff = math.sqrt(2.0 / math.pi)
    cube = 0.044715 * gate * gate
    hyper = jnp.tanh(coeff * (gate + cube * gate))
    half = 0.5 * (1.0 + hyper)
    act = gate * half
    slope = half + 0.5 * gate * (1.0 - hyper * hyper) * coeff * (1.0 + 3.0 * cube)
    grad_up = (grad_a * act).astype(BF16)
    grad_gate = (grad_a * up * slope).astype(BF16)
    center = jnp.sum(
        grad_gate.astype(F32) * gate + grad_up.astype(F32) * up, axis=0, keepdims=True
    )
    cen_out[...] = center
    high, low = split(center)
    out_scr[pl.ds(GROUP, 16), :] = rows_of(high, low, 16)
    grads[0:HID, :] = grad_gate
    grads[HID:, :] = grad_up
    near = grads[...]
    middle = HID // 2
    far_low = jnp.concatenate([grad_gate[:middle], grad_up[:middle]], axis=0)
    far_high = jnp.concatenate([grad_gate[middle:], grad_up[middle:]], axis=0)

    def backward(w, grad):
        return lax.dot_general(
            w[0:2].reshape(2 * w.shape[1], CHUNK),
            grad,
            (((0,), (0,)), ((), ())),
            preferred_element_type=F32,
        )

    for k, chunk in enumerate(chunks):
        if k < 3:
            part[...] = backward((w0, w1, w2)[k], near)
        else:
            part[...] = backward(w3, far_low) + backward(w4, far_high)
        for keep, send, parity in ((keep1, send1, 1 - odd), (keep2, send2, odd)):
            for s in range(N_Z // 2):
                base = (4 * s + 2 * parity) * PIECE
                mine = pl.multiple_of(base + core * PIECE, 8)
                theirs = pl.multiple_of(base + (1 - core) * PIECE, 8)
                keep[chunk, pl.ds(s * PIECE, PIECE), :] = part[pl.ds(mine, PIECE), :]
                out_scr[pl.ds(s * PIECE, PIECE), :] = part[pl.ds(theirs, PIECE), :]
            send[chunk] = out_scr[pl.ds(0, send.shape[1]), :].astype(BF16)


def core_sum_kernel(idx, keep1, keep2, got1, got2, cen, own1, own2, *refs):
    sends1, sends2, cen_out, scr = refs[:3], refs[3:6], refs[6], refs[7]
    tensor = idx[1]
    tail = got1[0].astype(F32)[GROUP:, :]
    center = cen[...] + tail[0:1, :] + tail[1:2, :]
    cen_out[...] = center
    high, low = split(center)
    scr[pl.ds(GROUP, 16), :] = rows_of(high, low, 16)
    own1[...] = keep1[tensor] + got1[tensor].astype(F32)[:GROUP, :]
    own2[...] = keep2[tensor] + got2[tensor].astype(F32)
    for e in (1, 2, 3):
        to = lax.rem(tensor + e, N_T)
        scr[pl.ds(0, GROUP), :] = keep1[to] + got1[to].astype(F32)[:GROUP, :]
        sends1[e - 1][...] = scr[...].astype(BF16)
        sends2[e - 1][...] = (keep2[to] + got2[to].astype(F32)).astype(BF16)


def tensor_sum_kernel(own, r1, r2, r3, cen, send, cen_out, scr):
    total = own[...]
    center = cen[...]
    for r in (r1, r2, r3):
        v = r[...].astype(F32)
        total = total + v[:GROUP, :]
        center = center + v[GROUP : GROUP + 1, :] + v[GROUP + 1 : GROUP + 2, :]
    cen_out[...] = center
    high, low = split(center)
    scr[pl.ds(0, GROUP), :] = total
    scr[pl.ds(GROUP, 16), :] = rows_of(high, low, 16)
    send[...] = scr[...].astype(BF16)


def pair_sum_kernel(own, r1, r2, r3, pair, cen, total_out, send, cen_out, scr):
    v = pair[...].astype(F32)
    total = own[...] + v[:GROUP, :]
    for r in (r1, r2, r3):
        total = total + r[...].astype(F32)
    center = cen[...] + v[GROUP : GROUP + 1, :] + v[GROUP + 1 : GROUP + 2, :]
    total_out[...] = total
    cen_out[...] = center
    high, low = split(center)
    scr[pl.ds(0, GROUP), :] = total
    scr[pl.ds(GROUP, 16), :] = rows_of(high, low, 16)
    send[...] = scr[...].astype(BF16)


def grad_kernel(idx, own, r1, r2, r3, cen, root, gain, bias, x_ref, g_ref, cast, err):
    total = own[...]
    center = cen[...]
    for r in (r1, r2, r3):
        v = r[...].astype(F32)
        total = total + v[:GROUP, :]
        center = center + v[GROUP : GROUP + 1, :] + v[GROUP + 1 : GROUP + 2, :]
    center = center * (1.0 / D)
    x = x_ref[...].astype(F32)
    inv = 1.0 / root[...]
    grad_x = g_ref[...].astype(F32) + (total * gain[...] - x * inv * center) * inv
    cast[...] = grad_x.astype(BF16)
    start = (idx[2] // 2) * PIECE
    index = lax.broadcasted_iota(jnp.int32, (GROUP, TOK), 0)
    mine = (index >= start) & (index < start + PIECE)
    terms = jnp.where(mine, grad_x * (x - bias[...]), 0.0)
    err[...] = jnp.sum(terms, axis=0, keepdims=True)


def fetch_kernel(ids, decoder, _, dec, passed, sems):
    copies = []
    for b in range(2):
        for r in range(CAP):
            rows = pl.ds(pl.multiple_of(ids[b, r] * BLOCK, BLOCK), BLOCK)
            copy = pltpu.make_async_copy(
                decoder.at[rows], dec.at[b, pl.ds(r * BLOCK, BLOCK)], sems.at[b, r]
            )
            copy.start()
            copies.append(copy)
    for copy in copies:
        copy.wait()


def stack_kernel(a, b, c, out, sems):
    copies = [pltpu.make_async_copy(w, out.at[i], sems.at[i]) for i, w in enumerate((a, b, c))]
    for copy in copies:
        copy.start()
    for copy in copies:
        copy.wait()


def decode_kernel(idx, g0, g1, g2, g3, err, dec, out, grad, scr):
    place = 2 * lax.rem(idx[2], 2) + idx[3]
    flips = (place, 2 * (1 - lax.rem(idx[2], 2)) + idx[3], 2 * lax.rem(idx[2], 2) + 1 - idx[3])
    last = 2 * (1 - lax.rem(idx[2], 2)) + 1 - idx[3]
    for g, at in zip((g0, g1, g2, g3), flips + (last,)):
        rows = g[...].astype(F32)
        for k in range(N_Z // 2):
            start = pl.multiple_of((4 * k + at) * PIECE, 8)
            scr[pl.ds(start, PIECE), :] = rows[k * PIECE : (k + 1) * PIECE, :]
    grad[...] = scr[...].astype(BF16)
    tall = jnp.broadcast_to(err[...], (BLOCK, TOK)).T
    high, low = split(tall)
    lane = lax.broadcasted_iota(jnp.int32, (TOK, BLOCK), 1)
    out[:, COLS:] = jnp.where(lane == 0, high, jnp.where(lane == 1, low, 0.0)).astype(BF16)
    for b in range(2):
        tokens = grad[:, b * BLOCK : (b + 1) * BLOCK]
        out[b * BLOCK : (b + 1) * BLOCK, :COLS] = lax.dot_general(
            tokens, dec[b], (((0,), (1,)), ((), ())), preferred_element_type=F32
        ).astype(BF16)


def score_kernel(slots, got, acts, scores, err, scr):
    for l in range(N_L):
        total = got[l].astype(F32)
        for t in range(1, N_T):
            total = total + got[t * N_L + l].astype(F32)
        scr[l] = total
    total = jnp.zeros((4, BLOCK), F32)
    for k in range(SLOTS):
        at = pl.ds(pl.multiple_of(slots[1, k] * BLOCK, BLOCK), BLOCK)
        live = slots[2, k].astype(F32)
        value = scr[slots[0, k], :, at] * (acts[:, k * BLOCK : (k + 1) * BLOCK].astype(F32) * live)
        total += value
        scores[:, k * BLOCK : (k + 1) * BLOCK] = value.astype(BF16)
    extra = jnp.sum(scr[:, :, COLS:], axis=0)
    rest = jnp.concatenate([extra - total, jnp.zeros((4, BLOCK), F32)], axis=0).T
    err[...] = jnp.sum(rest, axis=0, keepdims=True)[:, :4] * (1.0 / math.sqrt(D))


def on_device(
    resid,
    out_grad,
    norm_gain,
    w_gate,
    w_up,
    w_down_t,
    decoder,
    dec_bias,
    block_ids,
    counts,
    latent_acts,
):
    dp, tensor, latent = (lax.axis_index(a) for a in ("dp", "tensor", "latent"))
    idx = jnp.stack([dp, tensor, latent // 2, latent % 2]).astype(jnp.int32)

    with jax.named_scope("slots"):
        owner = block_ids // SLOTS
        same = owner[:, :, None] == owner[:, None, :]
        before = jnp.tril(jnp.ones((SLOTS, SLOTS), bool), -1)
        rank = jnp.sum(same & before, axis=2, dtype=jnp.int32)
        takes = (owner == latent)[:, :, None] & (rank[:, :, None] == jnp.arange(CAP))
        local = jnp.sum(jnp.where(takes, (block_ids % SLOTS)[:, :, None], 0), axis=1)
        token_block = tensor // 2
        live = jnp.arange(SLOTS, dtype=jnp.int32) < counts[token_block]
        slots = jnp.stack([owner[token_block], rank[token_block], live.astype(jnp.int32)])
    with jax.named_scope("weight_rows"):
        rows = call(
            stack_kernel,
            "stack",
            [HBM] * 3,
            shape((3, HID, CHUNK), BF16),
            [pltpu.SemaphoreType.DMA((3,))],
            limit=60,
        )(w_gate.T, w_up.T, w_down_t.T)
        below = shift(rows, "dp", N_DP, 1)
        above = shift(rows, "dp", N_DP, -1)
        middle = HID // 2
        far_low = shift(below[:, :middle], "dp", N_DP, 1)
        far_high = shift(above[:, middle:], "dp", N_DP, -1)

    with jax.named_scope("token_features"):
        x_own, g_own = resid.T, out_grad.T
        column = lax.all_gather(jnp.concatenate([x_own, g_own]), "latent", axis=0)
        x_all = column[:, :PIECE].reshape(CHUNK, TOK)
        g_all = column[:, PIECE:].reshape(CHUNK, TOK)
        fetch = jnp.where(latent % 2 == 0, x_all, g_all)
        own = [shift(fetch, "tensor", N_T, e) for e in range(1, N_T)]
        dec, own[0] = pl.pallas_call(
            fetch_kernel,
            name="fetch",
            in_specs=[SMEM, HBM, ANY],
            out_specs=(VMEM, ANY),
            out_shape=(shape((2, COLS, CHUNK), BF16), shape((CHUNK, TOK), BF16)),
            input_output_aliases={2: 1},
            scratch_shapes=[pltpu.SemaphoreType.DMA((2, CAP))],
            compiler_params=pltpu.CompilerParams(vmem_limit_bytes=8 * 2**20),
        )(local.astype(jnp.int32), decoder, own[0])
        other = [swap_core(a) for a in own]

    with jax.named_scope("mlp"):
        row = shape((1, TOK), F32)
        keep1, keep2, send1, send2, cen, root = call(
            mlp_kernel,
            "mlp",
            [SMEM] + [VMEM] * 14,
            (
                shape((N_T, GROUP, TOK), F32),
                shape((N_T, GROUP, TOK), F32),
                shape((N_T, SENT, TOK), BF16),
                shape((N_T, GROUP, TOK), BF16),
                row,
                row,
            ),
            [
                pltpu.VMEM((D, TOK), BF16),
                pltpu.VMEM((D, TOK), BF16),
                pltpu.VMEM((2 * HID, TOK), BF16),
                pltpu.VMEM((CHUNK, TOK), F32),
                pltpu.VMEM((SENT, TOK), F32),
            ],
            limit=26,
        )(
            idx, x_all, g_all, *own, *other, norm_gain.reshape(D // BLOCK, BLOCK),
            rows, below, above, far_low, far_high,
        )

    with jax.named_scope("hidden_sums"):
        tensor_shifts = (1, 2, 3)
        got1, got2 = swap_core(send1), swap_core(send2)
        group = shape((GROUP, TOK), F32)
        own1, own2, *sends, cen = call(
            core_sum_kernel,
            "core_sum",
            [SMEM] + [VMEM] * 5,
            (group, group)
            + (shape((SENT, TOK), BF16),) * 3
            + (shape((GROUP, TOK), BF16),) * 3
            + (row,),
            [pltpu.VMEM((SENT, TOK), F32)],
            limit=12,
        )(idx, keep1, keep2, got1, got2, cen)
        parts1 = [shift(s, "tensor", N_T, e) for e, s in zip(tensor_shifts, sends[:3])]
        parts2 = [shift(s, "tensor", N_T, e) for e, s in zip(tensor_shifts, sends[3:])]
        send, cen = call(
            tensor_sum_kernel,
            "tensor_sum",
            [VMEM] * 5,
            (shape((SENT, TOK), BF16), row),
            [pltpu.VMEM((SENT, TOK), F32)],
            limit=8,
        )(own1, *parts1, cen)
        pair = lax.ppermute(send, "latent", [(i, i ^ 2) for i in range(N_L)])
        total, send, cen = call(
            pair_sum_kernel,
            "pair_sum",
            [VMEM] * 6,
            (group, shape((SENT, TOK), BF16), row),
            [pltpu.VMEM((SENT, TOK), F32)],
            limit=8,
        )(own2, *parts2, pair, cen)
        got = [shift(send, "latent", N_L, 4 * d) for d in (1, 2, 3)]

        def group_rows(array):
            pieces = array.reshape(N_Z // 2, 4, PIECE, -1)
            return lax.dynamic_index_in_dim(pieces, latent % 4, 1, False).reshape(GROUP, -1)

        gain_own, bias_own = (
            group_rows(lax.dynamic_slice_in_dim(v, tensor * CHUNK, CHUNK, 0))
            for v in (norm_gain, dec_bias)
        )
        cast, err = call(
            grad_kernel,
            "grad",
            [SMEM] + [VMEM] * 10,
            (shape((GROUP, TOK), BF16), row),
            limit=8,
        )(idx, total, *got, cen, root, gain_own, bias_own, group_rows(x_all), group_rows(g_all))

    with jax.named_scope("decode"):
        across = lax.ppermute(cast, "latent", [(i, i ^ 2) for i in range(N_L)])
        products = call(
            decode_kernel,
            "decode",
            [SMEM] + [VMEM] * 6,
            shape((TOK, WIDE), BF16),
            [pltpu.VMEM((CHUNK, TOK), BF16), pltpu.VMEM((CHUNK, TOK), F32)],
            limit=14,
        )(idx, cast, across, swap_core(cast), swap_core(across), err, dec)

    with jax.named_scope("scores"):
        got = lax.all_to_all(
            products.reshape(N_T * N_L, 4, WIDE), ("tensor", "latent"), 0, 0, tiled=True
        )
        scores, err = call(
            score_kernel,
            "score",
            [SMEM, VMEM, VMEM],
            (shape((4, SLOTS * BLOCK), BF16), shape((1, 4), F32)),
            [pltpu.VMEM((N_L, 4, WIDE), F32)],
            limit=8,
        )(slots, got, latent_acts)
    return scores, err.reshape(4)


def solution(mesh):
    return jax.shard_map(
        on_device,
        mesh=mesh,
        in_specs=(
            P("dp", ("tensor", "latent")),
            P("dp", ("tensor", "latent")),
            P(),
            P("dp", ("tensor", "latent")),
            P("dp", ("tensor", "latent")),
            P("dp", ("tensor", "latent")),
            P("latent", "tensor"),
            P(),
            P("dp", None),
            P("dp"),
            P(("dp", "tensor", "latent"), None),
        ),
        out_specs=(P(("dp", "tensor", "latent"), None), P(("dp", "tensor", "latent"))),
        check_vma=False,
    )
```

```python
import functools
import math

import jax
import jax.numpy as jnp
from jax import lax
from jax.experimental import pallas as pl
from jax.experimental.pallas import tpu as pltpu
from jax.sharding import PartitionSpec as P

BLOCK = 128
N_DP, N_T, N_L, N_Z = 4, 4, 16, 8
TOK = 256
D = 3584
CHUNK = D // N_T
PIECE = CHUNK // N_L
HID = 224
HALF = CHUNK // 2
CAP = 8
SLOTS = 32
GROUP = HALF // 2
SENT = GROUP + 16
COLS = CAP * BLOCK
WIDE = COLS + BLOCK
OWN_TOK = TOK // N_T
EPS = 1e-06
F32, BF16 = jnp.float32, jnp.bfloat16

VMEM = pl.BlockSpec(memory_space=pltpu.VMEM)
SMEM = pl.BlockSpec(memory_space=pltpu.SMEM)
ANY = pl.BlockSpec(memory_space=pl.ANY)
HBM = pl.BlockSpec(memory_space=pltpu.HBM)


def shape(dims, dtype):
    return jax.ShapeDtypeStruct(dims, dtype)


def call(kernel, name, in_specs, outs, scratch=(), limit=48):
    return pl.pallas_call(
        kernel,
        name=name,
        in_specs=in_specs,
        out_specs=jax.tree.map(lambda _: VMEM, outs),
        out_shape=outs,
        scratch_shapes=list(scratch),
        compiler_params=pltpu.CompilerParams(vmem_limit_bytes=limit * 2**20),
    )


def shift(x, axis, size, by):
    return lax.ppermute(x, axis, [(i, (i + by) % size) for i in range(size)])


def swap_core(x):
    return lax.ppermute(x, "latent", [(i, i ^ 1) for i in range(N_L)])


def split(row):
    high = row.astype(BF16).astype(F32)
    return high, row - high


def rows_of(high, low, count):
    index = lax.broadcasted_iota(jnp.int32, (count, high.shape[1]), 0)
    return jnp.where(index == 0, high, jnp.where(index == 1, low, 0.0))


def mlp_kernel(idx, x0, g0, a1, a2, a3, b1, b2, b3, gain, w0, w1, w2, w3, w4, *refs):
    keep1, keep2, send1, send2, cen_out, root_out = refs[:6]
    x_scr, g_scr, grads, part, out_scr = refs[6:]
    dp, tensor, odd, core = idx[0], idx[1], lax.rem(idx[2], 2), idx[3]
    first = core == 0
    square = jnp.zeros((8, TOK), F32)
    for e, a, b in ((0, x0, g0), (1, a1, b1), (3, a2, b2), (2, a3, b3)):
        at = pl.ds(pl.multiple_of(lax.rem(tensor - e + N_T, N_T) * CHUNK, 16), CHUNK)
        va, vb = a[...], b[...]
        if e:
            va, vb = jnp.where(first, va, vb), jnp.where(first, vb, va)
        x_scr[at, :] = va
        g_scr[at, :] = vb
        x = va.astype(F32)
        square += jnp.sum((x * x).reshape(CHUNK // 8, 8, TOK), axis=0)
    mean = jnp.sum(square, axis=0, keepdims=True) * (1.0 / D)
    root = jnp.sqrt(mean + EPS)
    root_out[...] = root
    inv = 1.0 / root
    columns = gain[...].T
    for i in range(D // BLOCK):
        at = pl.ds(i * BLOCK, BLOCK)
        x_scr[at, :] = (x_scr[at, :].astype(F32) * inv * columns[:, i : i + 1]).astype(BF16)

    chunks = (dp, lax.rem(dp + N_DP - 1, N_DP), lax.rem(dp + 1, N_DP), lax.rem(dp + 2, N_DP))

    def forward(w, chunk):
        rows = w.shape[1]
        at = pl.ds(pl.multiple_of(chunk * CHUNK, 16), CHUNK)
        both = jnp.dot(
            w[0:2].reshape(2 * rows, CHUNK), x_scr[at, :], preferred_element_type=F32
        )
        down = jnp.dot(w[2], g_scr[at, :], preferred_element_type=F32)
        return both[:rows], both[rows:], down

    low, high = forward(w3, chunks[3]), forward(w4, chunks[3])
    sums = [jnp.concatenate(pair, axis=0) for pair in zip(low, high)]
    for w, chunk in ((w0, chunks[0]), (w1, chunks[1]), (w2, chunks[2])):
        sums = [total + v for total, v in zip(sums, forward(w, chunk))]
    gate, up, grad_a = sums
    coeff = math.sqrt(2.0 / math.pi)
    cube = 0.044715 * gate * gate
    hyper = jnp.tanh(coeff * (gate + cube * gate))
    half = 0.5 * (1.0 + hyper)
    act = gate * half
    slope = half + 0.5 * gate * (1.0 - hyper * hyper) * coeff * (1.0 + 3.0 * cube)
    grad_up = (grad_a * act).astype(BF16)
    grad_gate = (grad_a * up * slope).astype(BF16)
    center = jnp.sum(
        grad_gate.astype(F32) * gate + grad_up.astype(F32) * up, axis=0, keepdims=True
    )
    cen_out[...] = center
    high, low = split(center)
    out_scr[pl.ds(GROUP, 16), :] = rows_of(high, low, 16)
    grads[0:HID, :] = grad_gate
    grads[HID:, :] = grad_up
    near = grads[...]
    middle = HID // 2
    far_low = jnp.concatenate([grad_gate[:middle], grad_up[:middle]], axis=0)
    far_high = jnp.concatenate([grad_gate[middle:], grad_up[middle:]], axis=0)

    def backward(w, grad):
        return lax.dot_general(
            w[0:2].reshape(2 * w.shape[1], CHUNK),
            grad,
            (((0,), (0,)), ((), ())),
            preferred_element_type=F32,
        )

    for k, chunk in enumerate(chunks):
        if k < 3:
            part[...] = backward((w0, w1, w2)[k], near)
        else:
            part[...] = backward(w3, far_low) + backward(w4, far_high)
        for keep, send, parity in ((keep1, send1, 1 - odd), (keep2, send2, odd)):
            for s in range(N_Z // 2):
                base = (4 * s + 2 * parity) * PIECE
                mine = pl.multiple_of(base + core * PIECE, 8)
                theirs = pl.multiple_of(base + (1 - core) * PIECE, 8)
                keep[chunk, pl.ds(s * PIECE, PIECE), :] = part[pl.ds(mine, PIECE), :]
                out_scr[pl.ds(s * PIECE, PIECE), :] = part[pl.ds(theirs, PIECE), :]
            send[chunk] = out_scr[pl.ds(0, send.shape[1]), :].astype(BF16)


def core_sum_kernel(idx, keep1, keep2, got1, got2, cen, own1, own2, *refs):
    sends1, sends2, cen_out, scr = refs[:3], refs[3:6], refs[6], refs[7]
    tensor = idx[1]
    tail = got1[0].astype(F32)[GROUP:, :]
    center = cen[...] + tail[0:1, :] + tail[1:2, :]
    cen_out[...] = center
    high, low = split(center)
    scr[pl.ds(GROUP, 16), :] = rows_of(high, low, 16)
    own1[...] = keep1[tensor] + got1[tensor].astype(F32)[:GROUP, :]
    own2[...] = keep2[tensor] + got2[tensor].astype(F32)
    for e in (1, 2, 3):
        to = lax.rem(tensor + e, N_T)
        scr[pl.ds(0, GROUP), :] = keep1[to] + got1[to].astype(F32)[:GROUP, :]
        sends1[e - 1][...] = scr[...].astype(BF16)
        sends2[e - 1][...] = (keep2[to] + got2[to].astype(F32)).astype(BF16)


def tensor_sum_kernel(own, r1, r2, r3, cen, send, cen_out, scr):
    total = own[...]
    center = cen[...]
    for r in (r1, r2, r3):
        v = r[...].astype(F32)
        total = total + v[:GROUP, :]
        center = center + v[GROUP : GROUP + 1, :] + v[GROUP + 1 : GROUP + 2, :]
    cen_out[...] = center
    high, low = split(center)
    scr[pl.ds(0, GROUP), :] = total
    scr[pl.ds(GROUP, 16), :] = rows_of(high, low, 16)
    send[...] = scr[...].astype(BF16)


def pair_sum_kernel(own, r1, r2, r3, pair, cen, total_out, send, cen_out, scr):
    v = pair[...].astype(F32)
    total = own[...] + v[:GROUP, :]
    for r in (r1, r2, r3):
        total = total + r[...].astype(F32)
    center = cen[...] + v[GROUP : GROUP + 1, :] + v[GROUP + 1 : GROUP + 2, :]
    total_out[...] = total
    cen_out[...] = center
    high, low = split(center)
    scr[pl.ds(0, GROUP), :] = total
    scr[pl.ds(GROUP, 16), :] = rows_of(high, low, 16)
    send[...] = scr[...].astype(BF16)


def grad_kernel(idx, own, r1, r2, r3, cen, root, gain, bias, x_ref, g_ref, cast, err):
    total = own[...]
    center = cen[...]
    for r in (r1, r2, r3):
        v = r[...].astype(F32)
        total = total + v[:GROUP, :]
        center = center + v[GROUP : GROUP + 1, :] + v[GROUP + 1 : GROUP + 2, :]
    center = center * (1.0 / D)
    x = x_ref[...].astype(F32)
    inv = 1.0 / root[...]
    grad_x = g_ref[...].astype(F32) + (total * gain[...] - x * inv * center) * inv
    cast[...] = grad_x.astype(BF16)
    start = (idx[2] // 2) * PIECE
    index = lax.broadcasted_iota(jnp.int32, (GROUP, TOK), 0)
    mine = (index >= start) & (index < start + PIECE)
    terms = jnp.where(mine, grad_x * (x - bias[...]), 0.0)
    err[...] = jnp.sum(terms, axis=0, keepdims=True)


def fetch_kernel(ids, decoder, _, dec, passed, sems):
    def each(act):
        for b in range(2):
            for r in range(CAP):
                index = ids[b, r]

                @pl.when(index >= 0)
                def _():
                    rows = pl.ds(pl.multiple_of(jnp.maximum(index, 0) * BLOCK, BLOCK), BLOCK)
                    into = dec.at[b, pl.ds(r * BLOCK, BLOCK)]
                    act(pltpu.make_async_copy(decoder.at[rows], into, sems.at[b, r]))

    each(lambda copy: copy.start())
    each(lambda copy: copy.wait())


def stack_kernel(a, b, c, out, sems):
    copies = [pltpu.make_async_copy(w, out.at[i], sems.at[i]) for i, w in enumerate((a, b, c))]
    for copy in copies:
        copy.start()
    for copy in copies:
        copy.wait()


def decode_kernel(idx, g0, g1, g2, g3, err, dec, out, grad, scr):
    place = 2 * lax.rem(idx[2], 2) + idx[3]
    flips = (place, 2 * (1 - lax.rem(idx[2], 2)) + idx[3], 2 * lax.rem(idx[2], 2) + 1 - idx[3])
    last = 2 * (1 - lax.rem(idx[2], 2)) + 1 - idx[3]
    for g, at in zip((g0, g1, g2, g3), flips + (last,)):
        rows = g[...].astype(F32)
        for k in range(N_Z // 2):
            start = pl.multiple_of((4 * k + at) * PIECE, 8)
            scr[pl.ds(start, PIECE), :] = rows[k * PIECE : (k + 1) * PIECE, :]
    grad[...] = scr[...].astype(BF16)
    tall = jnp.broadcast_to(err[...], (BLOCK, TOK)).T
    high, low = split(tall)
    lane = lax.broadcasted_iota(jnp.int32, (TOK, BLOCK), 1)
    out[:, COLS:] = jnp.where(lane == 0, high, jnp.where(lane == 1, low, 0.0)).astype(BF16)
    for b in range(2):
        tokens = grad[:, b * BLOCK : (b + 1) * BLOCK]
        out[b * BLOCK : (b + 1) * BLOCK, :COLS] = lax.dot_general(
            tokens, dec[b], (((0,), (1,)), ((), ())), preferred_element_type=F32
        ).astype(BF16)


def score_kernel(slots, got, acts, scores, err, scr):
    for l in range(N_L):
        total = got[l].astype(F32)
        for t in range(1, N_T):
            total = total + got[t * N_L + l].astype(F32)
        scr[l] = total
    total = jnp.zeros((4, BLOCK), F32)
    for k in range(SLOTS):
        at = pl.ds(pl.multiple_of(slots[1, k] * BLOCK, BLOCK), BLOCK)
        value = scr[slots[0, k], :, at] * acts[:, k * BLOCK : (k + 1) * BLOCK].astype(F32)
        value = jnp.where(slots[2, k] > 0, value, 0.0)
        total += value
        scores[:, k * BLOCK : (k + 1) * BLOCK] = value.astype(BF16)
    extra = jnp.sum(scr[:, :, COLS:], axis=0)
    rest = jnp.concatenate([extra - total, jnp.zeros((4, BLOCK), F32)], axis=0).T
    err[...] = jnp.sum(rest, axis=0, keepdims=True)[:, :4] * (1.0 / math.sqrt(D))


def on_device(
    resid,
    out_grad,
    norm_gain,
    w_gate,
    w_up,
    w_down_t,
    decoder,
    dec_bias,
    block_ids,
    counts,
    latent_acts,
):
    dp, tensor, latent = (lax.axis_index(a) for a in ("dp", "tensor", "latent"))
    idx = jnp.stack([dp, tensor, latent // 2, latent % 2]).astype(jnp.int32)

    with jax.named_scope("slots"):
        owner = block_ids // SLOTS
        same = owner[:, :, None] == owner[:, None, :]
        before = jnp.tril(jnp.ones((SLOTS, SLOTS), bool), -1)
        rank = jnp.sum(same & before, axis=2, dtype=jnp.int32)
        live = jnp.arange(SLOTS, dtype=jnp.int32) < counts[:, None]
        mine = live & (owner == latent)
        takes = mine[:, :, None] & (rank[:, :, None] == jnp.arange(CAP))
        local = jnp.sum(jnp.where(takes, (block_ids % SLOTS)[:, :, None] + 1, 0), axis=1) - 1
        slots = jnp.stack([owner, rank, live.astype(jnp.int32)])[:, tensor // 2]
    with jax.named_scope("weight_rows"):
        rows = call(
            stack_kernel,
            "stack",
            [HBM] * 3,
            shape((3, HID, CHUNK), BF16),
            [pltpu.SemaphoreType.DMA((3,))],
            limit=60,
        )(w_gate.T, w_up.T, w_down_t.T)
        below = shift(rows, "dp", N_DP, 1)
        above = shift(rows, "dp", N_DP, -1)
        middle = HID // 2
        far_low = shift(below[:, :middle], "dp", N_DP, 1)
        far_high = shift(above[:, middle:], "dp", N_DP, -1)

    with jax.named_scope("token_features"):
        x_own, g_own = resid.T, out_grad.T
        column = lax.all_gather(jnp.concatenate([x_own, g_own]), "latent", axis=0)
        x_all = column[:, :PIECE].reshape(CHUNK, TOK)
        g_all = column[:, PIECE:].reshape(CHUNK, TOK)
        fetch = jnp.where(latent % 2 == 0, x_all, g_all)
        own = [shift(fetch, "tensor", N_T, e) for e in (1, 3, 2)]
        other = [swap_core(a) for a in own]

    with jax.named_scope("mlp"):
        row = shape((1, TOK), F32)
        keep1, keep2, send1, send2, cen, root = call(
            mlp_kernel,
            "mlp",
            [SMEM] + [VMEM] * 14,
            (
                shape((N_T, GROUP, TOK), F32),
                shape((N_T, GROUP, TOK), F32),
                shape((N_T, SENT, TOK), BF16),
                shape((N_T, GROUP, TOK), BF16),
                row,
                row,
            ),
            [
                pltpu.VMEM((D, TOK), BF16),
                pltpu.VMEM((D, TOK), BF16),
                pltpu.VMEM((2 * HID, TOK), BF16),
                pltpu.VMEM((CHUNK, TOK), F32),
                pltpu.VMEM((SENT, TOK), F32),
            ],
            limit=20,
        )(
            idx, x_all, g_all, *own, *other, norm_gain.reshape(D // BLOCK, BLOCK),
            rows, below, above, far_low, far_high,
        )

    with jax.named_scope("hidden_sums"):
        tensor_shifts = (1, 2, 3)
        got1, got2 = swap_core(send1), swap_core(send2)
        group = shape((GROUP, TOK), F32)
        own1, own2, *sends, cen = call(
            core_sum_kernel,
            "core_sum",
            [SMEM] + [VMEM] * 5,
            (group, group)
            + (shape((SENT, TOK), BF16),) * 3
            + (shape((GROUP, TOK), BF16),) * 3
            + (row,),
            [pltpu.VMEM((SENT, TOK), F32)],
            limit=12,
        )(idx, keep1, keep2, got1, got2, cen)
        parts1 = [shift(s, "tensor", N_T, e) for e, s in zip(tensor_shifts, sends[:3])]
        parts2 = [shift(s, "tensor", N_T, e) for e, s in zip(tensor_shifts, sends[3:])]
        send, cen = call(
            tensor_sum_kernel,
            "tensor_sum",
            [VMEM] * 5,
            (shape((SENT, TOK), BF16), row),
            [pltpu.VMEM((SENT, TOK), F32)],
            limit=8,
        )(own1, *parts1, cen)
        pair = lax.ppermute(send, "latent", [(i, i ^ 2) for i in range(N_L)])
        total, send, cen = call(
            pair_sum_kernel,
            "pair_sum",
            [VMEM] * 6,
            (group, shape((SENT, TOK), BF16), row),
            [pltpu.VMEM((SENT, TOK), F32)],
            limit=8,
        )(own2, *parts2, pair, cen)
        got = [shift(send, "latent", N_L, 4 * d) for d in (1, 2, 3)]

        dec, total = pl.pallas_call(
            fetch_kernel,
            name="fetch",
            in_specs=[SMEM, HBM, ANY],
            out_specs=(VMEM, ANY),
            out_shape=(shape((2, COLS, CHUNK), BF16), group),
            input_output_aliases={2: 1},
            scratch_shapes=[pltpu.SemaphoreType.DMA((2, CAP))],
            compiler_params=pltpu.CompilerParams(vmem_limit_bytes=8 * 2**20),
        )(local.astype(jnp.int32), decoder, total)

        def group_rows(array):
            pieces = array.reshape(N_Z // 2, 4, PIECE, -1)
            return lax.dynamic_index_in_dim(pieces, latent % 4, 1, False).reshape(GROUP, -1)

        gain_own, bias_own = (
            group_rows(lax.dynamic_slice_in_dim(v, tensor * CHUNK, CHUNK, 0))
            for v in (norm_gain, dec_bias)
        )
        cast, err = call(
            grad_kernel,
            "grad",
            [SMEM] + [VMEM] * 10,
            (shape((GROUP, TOK), BF16), row),
            limit=8,
        )(idx, total, *got, cen, root, gain_own, bias_own, group_rows(x_all), group_rows(g_all))

    with jax.named_scope("decode"):
        across = lax.ppermute(cast, "latent", [(i, i ^ 2) for i in range(N_L)])
        products = call(
            decode_kernel,
            "decode",
            [SMEM] + [VMEM] * 6,
            shape((TOK, WIDE), BF16),
            [pltpu.VMEM((CHUNK, TOK), BF16), pltpu.VMEM((CHUNK, TOK), F32)],
            limit=14,
        )(idx, cast, across, swap_core(cast), swap_core(across), err, dec)

    with jax.named_scope("scores"):
        got = lax.all_to_all(
            products.reshape(N_T * N_L, 4, WIDE), ("tensor", "latent"), 0, 0, tiled=True
        )
        scores, err = call(
            score_kernel,
            "score",
            [SMEM, VMEM, VMEM],
            (shape((4, SLOTS * BLOCK), BF16), shape((1, 4), F32)),
            [pltpu.VMEM((N_L, 4, WIDE), F32)],
            limit=8,
        )(slots, got, latent_acts)
    return scores, err.reshape(4)


def solution(mesh):
    return jax.shard_map(
        on_device,
        mesh=mesh,
        in_specs=(
            P("dp", ("tensor", "latent")),
            P("dp", ("tensor", "latent")),
            P(),
            P("dp", ("tensor", "latent")),
            P("dp", ("tensor", "latent")),
            P("dp", ("tensor", "latent")),
            P("latent", "tensor"),
            P(),
            P("dp", None),
            P("dp"),
            P(("dp", "tensor", "latent"), None),
        ),
        out_specs=(P(("dp", "tensor", "latent"), None), P(("dp", "tensor", "latent"))),
        check_vma=False,
    )
```

```python
import functools
import math

import jax
import jax.numpy as jnp
from jax import lax
from jax.experimental import pallas as pl
from jax.experimental.pallas import tpu as pltpu
from jax.sharding import PartitionSpec as P

BLOCK = 128
N_DP, N_T, N_L, N_Z = 4, 4, 16, 8
TOK = 256
D = 3584
CHUNK = D // N_T
PIECE = CHUNK // N_L
HID = 224
HALF = CHUNK // 2
CAP = 8
SLOTS = 32
GROUP = HALF // 2
SENT = GROUP + 16
COLS = CAP * BLOCK
WIDE = COLS + BLOCK
OWN_TOK = TOK // N_T
EPS = 1e-06
F32, BF16 = jnp.float32, jnp.bfloat16

VMEM = pl.BlockSpec(memory_space=pltpu.VMEM)
SMEM = pl.BlockSpec(memory_space=pltpu.SMEM)
ANY = pl.BlockSpec(memory_space=pl.ANY)
HBM = pl.BlockSpec(memory_space=pltpu.HBM)


def shape(dims, dtype):
    return jax.ShapeDtypeStruct(dims, dtype)


def call(kernel, name, in_specs, outs, scratch=(), limit=48):
    return pl.pallas_call(
        kernel,
        name=name,
        in_specs=in_specs,
        out_specs=jax.tree.map(lambda _: VMEM, outs),
        out_shape=outs,
        scratch_shapes=list(scratch),
        compiler_params=pltpu.CompilerParams(vmem_limit_bytes=limit * 2**20),
    )


def shift(x, axis, size, by):
    return lax.ppermute(x, axis, [(i, (i + by) % size) for i in range(size)])


def swap_core(x):
    return lax.ppermute(x, "latent", [(i, i ^ 1) for i in range(N_L)])


def split(row):
    high = row.astype(BF16).astype(F32)
    return high, row - high


def rows_of(high, low, count):
    index = lax.broadcasted_iota(jnp.int32, (count, high.shape[1]), 0)
    return jnp.where(index == 0, high, jnp.where(index == 1, low, 0.0))


def mlp_kernel(idx, x0, g0, a1, a2, a3, b1, b2, b3, gain, w0, w1, w2, w3, w4, *refs):
    keep1, keep2, send1, send2, cen_out, root_out = refs[:6]
    x_scr, g_scr, grads, part, out_scr = refs[6:]
    dp, tensor, odd, core = idx[0], idx[1], lax.rem(idx[2], 2), idx[3]
    first = core == 0
    square = jnp.zeros((8, TOK), F32)
    for e, a, b in ((0, x0, g0), (1, a1, b1), (3, a2, b2), (2, a3, b3)):
        at = pl.ds(pl.multiple_of(lax.rem(tensor - e + N_T, N_T) * CHUNK, 16), CHUNK)
        va, vb = a[...], b[...]
        if e:
            va, vb = jnp.where(first, va, vb), jnp.where(first, vb, va)
        x_scr[at, :] = va
        g_scr[at, :] = vb
        x = va.astype(F32)
        square += jnp.sum((x * x).reshape(CHUNK // 8, 8, TOK), axis=0)
    mean = jnp.sum(square, axis=0, keepdims=True) * (1.0 / D)
    root = jnp.sqrt(mean + EPS)
    root_out[...] = root
    inv = 1.0 / root
    columns = gain[...].T
    for i in range(D // BLOCK):
        at = pl.ds(i * BLOCK, BLOCK)
        x_scr[at, :] = (x_scr[at, :].astype(F32) * inv * columns[:, i : i + 1]).astype(BF16)

    chunks = (dp, lax.rem(dp + N_DP - 1, N_DP), lax.rem(dp + 1, N_DP), lax.rem(dp + 2, N_DP))

    def forward(w, chunk):
        rows = w.shape[1]
        at = pl.ds(pl.multiple_of(chunk * CHUNK, 16), CHUNK)
        both = jnp.dot(
            w[0:2].reshape(2 * rows, CHUNK), x_scr[at, :], preferred_element_type=F32
        )
        down = jnp.dot(w[2], g_scr[at, :], preferred_element_type=F32)
        return both[:rows], both[rows:], down

    low, high = forward(w3, chunks[3]), forward(w4, chunks[3])
    sums = [jnp.concatenate(pair, axis=0) for pair in zip(low, high)]
    for w, chunk in ((w0, chunks[0]), (w1, chunks[1]), (w2, chunks[2])):
        sums = [total + v for total, v in zip(sums, forward(w, chunk))]
    gate, up, grad_a = sums
    coeff = math.sqrt(2.0 / math.pi)
    cube = 0.044715 * gate * gate
    hyper = jnp.tanh(coeff * (gate + cube * gate))
    half = 0.5 * (1.0 + hyper)
    act = gate * half
    slope = half + 0.5 * gate * (1.0 - hyper * hyper) * coeff * (1.0 + 3.0 * cube)
    grad_up = (grad_a * act).astype(BF16)
    grad_gate = (grad_a * up * slope).astype(BF16)
    center = jnp.sum(
        grad_gate.astype(F32) * gate + grad_up.astype(F32) * up, axis=0, keepdims=True
    )
    cen_out[...] = center
    high, low = split(center)
    out_scr[pl.ds(GROUP, 16), :] = rows_of(high, low, 16)
    grads[0:HID, :] = grad_gate
    grads[HID:, :] = grad_up
    near = grads[...]
    middle = HID // 2
    far_low = jnp.concatenate([grad_gate[:middle], grad_up[:middle]], axis=0)
    far_high = jnp.concatenate([grad_gate[middle:], grad_up[middle:]], axis=0)

    def backward(w, grad):
        return lax.dot_general(
            w[0:2].reshape(2 * w.shape[1], CHUNK),
            grad,
            (((0,), (0,)), ((), ())),
            preferred_element_type=F32,
        )

    for k, chunk in enumerate(chunks):
        if k < 3:
            part[...] = backward((w0, w1, w2)[k], near)
        else:
            part[...] = backward(w3, far_low) + backward(w4, far_high)
        for keep, send, parity in ((keep1, send1, 1 - odd), (keep2, send2, odd)):
            for s in range(N_Z // 2):
                base = (4 * s + 2 * parity) * PIECE
                mine = pl.multiple_of(base + core * PIECE, 8)
                theirs = pl.multiple_of(base + (1 - core) * PIECE, 8)
                keep[chunk, pl.ds(s * PIECE, PIECE), :] = part[pl.ds(mine, PIECE), :]
                out_scr[pl.ds(s * PIECE, PIECE), :] = part[pl.ds(theirs, PIECE), :]
            send[chunk] = out_scr[pl.ds(0, send.shape[1]), :].astype(BF16)


def core_sum_kernel(idx, keep1, keep2, got1, got2, cen, own1, own2, *refs):
    sends1, sends2, cen_out, scr = refs[:3], refs[3:6], refs[6], refs[7]
    tensor = idx[1]
    tail = got1[0].astype(F32)[GROUP:, :]
    center = cen[...] + tail[0:1, :] + tail[1:2, :]
    cen_out[...] = center
    high, low = split(center)
    scr[pl.ds(GROUP, 16), :] = rows_of(high, low, 16)
    own1[...] = keep1[tensor] + got1[tensor].astype(F32)[:GROUP, :]
    own2[...] = keep2[tensor] + got2[tensor].astype(F32)
    for e in (1, 2, 3):
        to = lax.rem(tensor + e, N_T)
        scr[pl.ds(0, GROUP), :] = keep1[to] + got1[to].astype(F32)[:GROUP, :]
        sends1[e - 1][...] = scr[...].astype(BF16)
        sends2[e - 1][...] = (keep2[to] + got2[to].astype(F32)).astype(BF16)


def tensor_sum_kernel(own, r1, r2, r3, cen, send, cen_out, scr):
    total = own[...]
    center = cen[...]
    for r in (r1, r2, r3):
        v = r[...].astype(F32)
        total = total + v[:GROUP, :]
        center = center + v[GROUP : GROUP + 1, :] + v[GROUP + 1 : GROUP + 2, :]
    cen_out[...] = center
    high, low = split(center)
    scr[pl.ds(0, GROUP), :] = total
    scr[pl.ds(GROUP, 16), :] = rows_of(high, low, 16)
    send[...] = scr[...].astype(BF16)


def pair_sum_kernel(own, r1, r2, r3, pair, cen, total_out, send, cen_out, scr):
    v = pair[...].astype(F32)
    total = own[...] + v[:GROUP, :]
    for r in (r1, r2, r3):
        total = total + r[...].astype(F32)
    center = cen[...] + v[GROUP : GROUP + 1, :] + v[GROUP + 1 : GROUP + 2, :]
    total_out[...] = total
    cen_out[...] = center
    high, low = split(center)
    scr[pl.ds(0, GROUP), :] = total
    scr[pl.ds(GROUP, 16), :] = rows_of(high, low, 16)
    send[...] = scr[...].astype(BF16)


def grad_kernel(idx, own, r1, r2, r3, cen, root, gain, bias, x_ref, g_ref, cast, err):
    total = own[...]
    center = cen[...]
    for r in (r1, r2, r3):
        v = r[...].astype(F32)
        total = total + v[:GROUP, :]
        center = center + v[GROUP : GROUP + 1, :] + v[GROUP + 1 : GROUP + 2, :]
    center = center * (1.0 / D)
    x = x_ref[...].astype(F32)
    inv = 1.0 / root[...]
    grad_x = g_ref[...].astype(F32) + (total * gain[...] - x * inv * center) * inv
    cast[...] = grad_x.astype(BF16)
    start = (idx[2] // 2) * PIECE
    index = lax.broadcasted_iota(jnp.int32, (GROUP, TOK), 0)
    mine = (index >= start) & (index < start + PIECE)
    terms = jnp.where(mine, grad_x * (x - bias[...]), 0.0)
    err[...] = jnp.sum(terms, axis=0, keepdims=True)


def fetch_kernel(ids, decoder, _, dec, passed, sems):
    def each(act):
        for b in range(2):
            for r in range(CAP):
                index = ids[b, r]

                @pl.when(index >= 0)
                def _():
                    rows = pl.ds(pl.multiple_of(jnp.maximum(index, 0) * BLOCK, BLOCK), BLOCK)
                    into = dec.at[b, pl.ds(r * BLOCK, BLOCK)]
                    act(pltpu.make_async_copy(decoder.at[rows], into, sems.at[b, r]))

    each(lambda copy: copy.start())
    each(lambda copy: copy.wait())


def stack_kernel(a, b, c, out, sems):
    copies = [pltpu.make_async_copy(w, out.at[i], sems.at[i]) for i, w in enumerate((a, b, c))]
    for copy in copies:
        copy.start()
    for copy in copies:
        copy.wait()


def decode_kernel(idx, g0, g1, g2, g3, err, dec, own, s1, s2, s3, grad, scr, wide):
    place = 2 * lax.rem(idx[2], 2) + idx[3]
    flips = (place, 2 * (1 - lax.rem(idx[2], 2)) + idx[3], 2 * lax.rem(idx[2], 2) + 1 - idx[3])
    last = 2 * (1 - lax.rem(idx[2], 2)) + 1 - idx[3]
    for g, at in zip((g0, g1, g2, g3), flips + (last,)):
        rows = g[...].astype(F32)
        for k in range(N_Z // 2):
            start = pl.multiple_of((4 * k + at) * PIECE, 8)
            scr[pl.ds(start, PIECE), :] = rows[k * PIECE : (k + 1) * PIECE, :]
    grad[...] = scr[...].astype(BF16)
    tall = jnp.broadcast_to(err[...], (BLOCK, TOK)).T
    high, low = split(tall)
    lane = lax.broadcasted_iota(jnp.int32, (TOK, BLOCK), 1)
    wide[:, COLS:] = jnp.where(lane == 0, high, jnp.where(lane == 1, low, 0.0))
    for b in range(2):
        tokens = grad[:, b * BLOCK : (b + 1) * BLOCK]
        wide[b * BLOCK : (b + 1) * BLOCK, :COLS] = lax.dot_general(
            tokens, dec[b], (((0,), (1,)), ((), ())), preferred_element_type=F32
        )
    tensor = idx[1]
    own[...] = wide[pl.ds(pl.multiple_of(tensor * OWN_TOK, OWN_TOK), OWN_TOK), :]
    for e, out in ((1, s1), (2, s2), (3, s3)):
        to = lax.rem(tensor + e, N_T)
        rows = pl.ds(pl.multiple_of(to * OWN_TOK, OWN_TOK), OWN_TOK)
        out[...] = wide[rows, :].astype(BF16)


def product_sum_kernel(own, r1, r2, r3, out):
    total = own[...]
    for r in (r1, r2, r3):
        total = total + r[...].astype(F32)
    out[:, :COLS] = total[:, :COLS].astype(BF16)
    high, low = split(total[:, COLS : COLS + 1] + total[:, COLS + 1 : COLS + 2])
    lane = lax.broadcasted_iota(jnp.int32, (OWN_TOK, BLOCK), 1)
    out[:, COLS:] = jnp.where(lane == 0, high, jnp.where(lane == 1, low, 0.0)).astype(BF16)


def score_kernel(slots, got, acts, scores, err, scr):
    scr[...] = got[...].astype(F32)
    total = jnp.zeros((4, BLOCK), F32)
    for k in range(SLOTS):
        at = pl.ds(pl.multiple_of(slots[1, k] * BLOCK, BLOCK), BLOCK)
        value = scr[slots[0, k], :, at] * acts[:, k * BLOCK : (k + 1) * BLOCK].astype(F32)
        value = jnp.where(slots[2, k] > 0, value, 0.0)
        total += value
        scores[:, k * BLOCK : (k + 1) * BLOCK] = value.astype(BF16)
    extra = jnp.sum(scr[:, :, COLS:], axis=0)
    rest = jnp.concatenate([extra - total, jnp.zeros((4, BLOCK), F32)], axis=0).T
    err[...] = jnp.sum(rest, axis=0, keepdims=True)[:, :4] * (1.0 / math.sqrt(D))


def on_device(
    resid,
    out_grad,
    norm_gain,
    w_gate,
    w_up,
    w_down_t,
    decoder,
    dec_bias,
    block_ids,
    counts,
    latent_acts,
):
    dp, tensor, latent = (lax.axis_index(a) for a in ("dp", "tensor", "latent"))
    idx = jnp.stack([dp, tensor, latent // 2, latent % 2]).astype(jnp.int32)

    with jax.named_scope("slots"):
        owner = block_ids // SLOTS
        same = owner[:, :, None] == owner[:, None, :]
        before = jnp.tril(jnp.ones((SLOTS, SLOTS), bool), -1)
        rank = jnp.sum(same & before, axis=2, dtype=jnp.int32)
        live = jnp.arange(SLOTS, dtype=jnp.int32) < counts[:, None]
        mine = live & (owner == latent)
        takes = mine[:, :, None] & (rank[:, :, None] == jnp.arange(CAP))
        local = jnp.sum(jnp.where(takes, (block_ids % SLOTS)[:, :, None] + 1, 0), axis=1) - 1
        slots = jnp.stack([owner, rank, live.astype(jnp.int32)])[:, tensor // 2]
    with jax.named_scope("weight_rows"):
        rows = call(
            stack_kernel,
            "stack",
            [HBM] * 3,
            shape((3, HID, CHUNK), BF16),
            [pltpu.SemaphoreType.DMA((3,))],
            limit=60,
        )(w_gate.T, w_up.T, w_down_t.T)
        below = shift(rows, "dp", N_DP, 1)
        above = shift(rows, "dp", N_DP, -1)
        middle = HID // 2
        far_low = shift(below[:, :middle], "dp", N_DP, 1)
        far_high = shift(above[:, middle:], "dp", N_DP, -1)

    with jax.named_scope("token_features"):
        x_own, g_own = resid.T, out_grad.T
        column = lax.all_gather(jnp.concatenate([x_own, g_own]), "latent", axis=0)
        x_all = column[:, :PIECE].reshape(CHUNK, TOK)
        g_all = column[:, PIECE:].reshape(CHUNK, TOK)
        fetch = jnp.where(latent % 2 == 0, x_all, g_all)
        own = [shift(fetch, "tensor", N_T, e) for e in (1, 3, 2)]
        other = [swap_core(a) for a in own]

    with jax.named_scope("mlp"):
        row = shape((1, TOK), F32)
        keep1, keep2, send1, send2, cen, root = call(
            mlp_kernel,
            "mlp",
            [SMEM] + [VMEM] * 14,
            (
                shape((N_T, GROUP, TOK), F32),
                shape((N_T, GROUP, TOK), F32),
                shape((N_T, SENT, TOK), BF16),
                shape((N_T, GROUP, TOK), BF16),
                row,
                row,
            ),
            [
                pltpu.VMEM((D, TOK), BF16),
                pltpu.VMEM((D, TOK), BF16),
                pltpu.VMEM((2 * HID, TOK), BF16),
                pltpu.VMEM((CHUNK, TOK), F32),
                pltpu.VMEM((SENT, TOK), F32),
            ],
            limit=20,
        )(
            idx, x_all, g_all, *own, *other, norm_gain.reshape(D // BLOCK, BLOCK),
            rows, below, above, far_low, far_high,
        )

    with jax.named_scope("hidden_sums"):
        tensor_shifts = (1, 2, 3)
        got1, got2 = swap_core(send1), swap_core(send2)
        group = shape((GROUP, TOK), F32)
        own1, own2, *sends, cen = call(
            core_sum_kernel,
            "core_sum",
            [SMEM] + [VMEM] * 5,
            (group, group)
            + (shape((SENT, TOK), BF16),) * 3
            + (shape((GROUP, TOK), BF16),) * 3
            + (row,),
            [pltpu.VMEM((SENT, TOK), F32)],
            limit=12,
        )(idx, keep1, keep2, got1, got2, cen)
        parts1 = [shift(s, "tensor", N_T, e) for e, s in zip(tensor_shifts, sends[:3])]
        parts2 = [shift(s, "tensor", N_T, e) for e, s in zip(tensor_shifts, sends[3:])]
        send, cen = call(
            tensor_sum_kernel,
            "tensor_sum",
            [VMEM] * 5,
            (shape((SENT, TOK), BF16), row),
            [pltpu.VMEM((SENT, TOK), F32)],
            limit=8,
        )(own1, *parts1, cen)
        pair = lax.ppermute(send, "latent", [(i, i ^ 2) for i in range(N_L)])
        total, send, cen = call(
            pair_sum_kernel,
            "pair_sum",
            [VMEM] * 6,
            (group, shape((SENT, TOK), BF16), row),
            [pltpu.VMEM((SENT, TOK), F32)],
            limit=8,
        )(own2, *parts2, pair, cen)
        got = [shift(send, "latent", N_L, 4 * d) for d in (1, 2, 3)]

        dec, total = pl.pallas_call(
            fetch_kernel,
            name="fetch",
            in_specs=[SMEM, HBM, ANY],
            out_specs=(VMEM, ANY),
            out_shape=(shape((2, COLS, CHUNK), BF16), group),
            input_output_aliases={2: 1},
            scratch_shapes=[pltpu.SemaphoreType.DMA((2, CAP))],
            compiler_params=pltpu.CompilerParams(vmem_limit_bytes=8 * 2**20),
        )(local.astype(jnp.int32), decoder, total)

        def group_rows(array):
            pieces = array.reshape(N_Z // 2, 4, PIECE, -1)
            return lax.dynamic_index_in_dim(pieces, latent % 4, 1, False).reshape(GROUP, -1)

        gain_own, bias_own = (
            group_rows(lax.dynamic_slice_in_dim(v, tensor * CHUNK, CHUNK, 0))
            for v in (norm_gain, dec_bias)
        )
        cast, err = call(
            grad_kernel,
            "grad",
            [SMEM] + [VMEM] * 10,
            (shape((GROUP, TOK), BF16), row),
            limit=8,
        )(idx, total, *got, cen, root, gain_own, bias_own, group_rows(x_all), group_rows(g_all))

    with jax.named_scope("decode"):
        across = lax.ppermute(cast, "latent", [(i, i ^ 2) for i in range(N_L)])
        kept, *sends = call(
            decode_kernel,
            "decode",
            [SMEM] + [VMEM] * 6,
            (shape((OWN_TOK, WIDE), F32),) + (shape((OWN_TOK, WIDE), BF16),) * 3,
            [
                pltpu.VMEM((CHUNK, TOK), BF16),
                pltpu.VMEM((CHUNK, TOK), F32),
                pltpu.VMEM((TOK, WIDE), F32),
            ],
            limit=14,
        )(idx, cast, across, swap_core(cast), swap_core(across), err, dec)

        moved = [shift(s, "tensor", N_T, e) for e, s in zip(tensor_shifts, sends)]
        products = call(
            product_sum_kernel, "product_sum", [VMEM] * 4, shape((OWN_TOK, WIDE), BF16), limit=8
        )(kept, *moved)

    with jax.named_scope("scores"):
        got = lax.all_to_all(products.reshape(N_L, 4, WIDE), "latent", 0, 0, tiled=True)
        scores, err = call(
            score_kernel,
            "score",
            [SMEM, VMEM, VMEM],
            (shape((4, SLOTS * BLOCK), BF16), shape((1, 4), F32)),
            [pltpu.VMEM((N_L, 4, WIDE), F32)],
            limit=8,
        )(slots, got, latent_acts)
    return scores, err.reshape(4)


def solution(mesh):
    return jax.shard_map(
        on_device,
        mesh=mesh,
        in_specs=(
            P("dp", ("tensor", "latent")),
            P("dp", ("tensor", "latent")),
            P(),
            P("dp", ("tensor", "latent")),
            P("dp", ("tensor", "latent")),
            P("dp", ("tensor", "latent")),
            P("latent", "tensor"),
            P(),
            P("dp", None),
            P("dp"),
            P(("dp", "tensor", "latent"), None),
        ),
        out_specs=(P(("dp", "tensor", "latent"), None), P(("dp", "tensor", "latent"))),
        check_vma=False,
    )
```

```python
import functools
import math

import jax
import jax.numpy as jnp
from jax import lax
from jax.experimental import pallas as pl
from jax.experimental.pallas import tpu as pltpu
from jax.sharding import PartitionSpec as P

BLOCK = 128
N_DP, N_T, N_L, N_Z = 4, 4, 16, 8
TOK = 256
D = 3584
CHUNK = D // N_T
PIECE = CHUNK // N_L
HID = 224
HALF = CHUNK // 2
CAP = 8
SLOTS = 32
GROUP = HALF // 2
SENT = GROUP + 16
COLS = CAP * BLOCK
WIDE = COLS + BLOCK
OWN_TOK = TOK // N_T
EPS = 1e-06
F32, BF16 = jnp.float32, jnp.bfloat16

VMEM = pl.BlockSpec(memory_space=pltpu.VMEM)
SMEM = pl.BlockSpec(memory_space=pltpu.SMEM)
ANY = pl.BlockSpec(memory_space=pl.ANY)
HBM = pl.BlockSpec(memory_space=pltpu.HBM)


def shape(dims, dtype):
    return jax.ShapeDtypeStruct(dims, dtype)


def call(kernel, name, in_specs, outs, scratch=(), limit=48):
    return pl.pallas_call(
        kernel,
        name=name,
        in_specs=in_specs,
        out_specs=jax.tree.map(lambda _: VMEM, outs),
        out_shape=outs,
        scratch_shapes=list(scratch),
        compiler_params=pltpu.CompilerParams(vmem_limit_bytes=limit * 2**20),
    )


def shift(x, axis, size, by):
    return lax.ppermute(x, axis, [(i, (i + by) % size) for i in range(size)])


def swap_core(x):
    return lax.ppermute(x, "latent", [(i, i ^ 1) for i in range(N_L)])


def split(row):
    high = row.astype(BF16).astype(F32)
    return high, row - high


def rows_of(high, low, count):
    index = lax.broadcasted_iota(jnp.int32, (count, high.shape[1]), 0)
    return jnp.where(index == 0, high, jnp.where(index == 1, low, 0.0))


def early_kernel(idx, x0, g0, a1, a2, b1, b2, x_out, g_out, square_out):
    tensor, core = idx[1], idx[3]
    first = core == 0
    square = jnp.zeros((8, TOK), F32)
    for e, a, b in ((0, x0, g0), (1, a1, b1), (3, a2, b2)):
        at = pl.ds(pl.multiple_of(lax.rem(tensor - e + N_T, N_T) * CHUNK, 16), CHUNK)
        va, vb = a[...], b[...]
        if e:
            va, vb = jnp.where(first, va, vb), jnp.where(first, vb, va)
        x_out[at, :] = va
        g_out[at, :] = vb
        x = va.astype(F32)
        square += jnp.sum((x * x).reshape(CHUNK // 8, 8, TOK), axis=0)
    square_out[...] = square


def mlp_kernel(idx, x_in, g_in, square_in, a3, b3, gain, w0, w1, w2, w3, w4, *refs):
    keep1, keep2, send1, send2, cen_out, root_out = refs[:6]
    x_scr, g_scr, grads, part, out_scr = refs[6:]
    dp, tensor, odd, core = idx[0], idx[1], lax.rem(idx[2], 2), idx[3]
    first = core == 0
    x_scr[...] = x_in[...]
    g_scr[...] = g_in[...]
    at = pl.ds(pl.multiple_of(lax.rem(tensor + 2, N_T) * CHUNK, 16), CHUNK)
    va, vb = a3[...], b3[...]
    va, vb = jnp.where(first, va, vb), jnp.where(first, vb, va)
    x_scr[at, :] = va
    g_scr[at, :] = vb
    x = va.astype(F32)
    square = square_in[...] + jnp.sum((x * x).reshape(CHUNK // 8, 8, TOK), axis=0)
    mean = jnp.sum(square, axis=0, keepdims=True) * (1.0 / D)
    root = jnp.sqrt(mean + EPS)
    root_out[...] = root
    inv = 1.0 / root
    columns = gain[...].T
    for i in range(D // BLOCK):
        at = pl.ds(i * BLOCK, BLOCK)
        x_scr[at, :] = (x_scr[at, :].astype(F32) * inv * columns[:, i : i + 1]).astype(BF16)

    chunks = (dp, lax.rem(dp + N_DP - 1, N_DP), lax.rem(dp + 1, N_DP), lax.rem(dp + 2, N_DP))

    def forward(w, chunk):
        rows = w.shape[1]
        at = pl.ds(pl.multiple_of(chunk * CHUNK, 16), CHUNK)
        both = jnp.dot(
            w[0:2].reshape(2 * rows, CHUNK), x_scr[at, :], preferred_element_type=F32
        )
        down = jnp.dot(w[2], g_scr[at, :], preferred_element_type=F32)
        return both[:rows], both[rows:], down

    low, high = forward(w3, chunks[3]), forward(w4, chunks[3])
    sums = [jnp.concatenate(pair, axis=0) for pair in zip(low, high)]
    for w, chunk in ((w0, chunks[0]), (w1, chunks[1]), (w2, chunks[2])):
        sums = [total + v for total, v in zip(sums, forward(w, chunk))]
    gate, up, grad_a = sums
    coeff = math.sqrt(2.0 / math.pi)
    cube = 0.044715 * gate * gate
    hyper = jnp.tanh(coeff * (gate + cube * gate))
    half = 0.5 * (1.0 + hyper)
    act = gate * half
    slope = half + 0.5 * gate * (1.0 - hyper * hyper) * coeff * (1.0 + 3.0 * cube)
    grad_up = (grad_a * act).astype(BF16)
    grad_gate = (grad_a * up * slope).astype(BF16)
    center = jnp.sum(
        grad_gate.astype(F32) * gate + grad_up.astype(F32) * up, axis=0, keepdims=True
    )
    cen_out[...] = center
    high, low = split(center)
    out_scr[pl.ds(GROUP, 16), :] = rows_of(high, low, 16)
    grads[0:HID, :] = grad_gate
    grads[HID:, :] = grad_up
    near = grads[...]
    middle = HID // 2
    far_low = jnp.concatenate([grad_gate[:middle], grad_up[:middle]], axis=0)
    far_high = jnp.concatenate([grad_gate[middle:], grad_up[middle:]], axis=0)

    def backward(w, grad):
        return lax.dot_general(
            w[0:2].reshape(2 * w.shape[1], CHUNK),
            grad,
            (((0,), (0,)), ((), ())),
            preferred_element_type=F32,
        )

    for k, chunk in enumerate(chunks):
        if k < 3:
            part[...] = backward((w0, w1, w2)[k], near)
        else:
            part[...] = backward(w3, far_low) + backward(w4, far_high)
        for keep, send, parity in ((keep1, send1, 1 - odd), (keep2, send2, odd)):
            for s in range(N_Z // 2):
                base = (4 * s + 2 * parity) * PIECE
                mine = pl.multiple_of(base + core * PIECE, 8)
                theirs = pl.multiple_of(base + (1 - core) * PIECE, 8)
                keep[chunk, pl.ds(s * PIECE, PIECE), :] = part[pl.ds(mine, PIECE), :]
                out_scr[pl.ds(s * PIECE, PIECE), :] = part[pl.ds(theirs, PIECE), :]
            send[chunk] = out_scr[pl.ds(0, send.shape[1]), :].astype(BF16)


def core_sum_kernel(idx, keep1, keep2, got1, got2, cen, own1, own2, *refs):
    sends1, sends2, cen_out, scr = refs[:3], refs[3:6], refs[6], refs[7]
    tensor = idx[1]
    tail = got1[0].astype(F32)[GROUP:, :]
    center = cen[...] + tail[0:1, :] + tail[1:2, :]
    cen_out[...] = center
    high, low = split(center)
    scr[pl.ds(GROUP, 16), :] = rows_of(high, low, 16)
    own1[...] = keep1[tensor] + got1[tensor].astype(F32)[:GROUP, :]
    own2[...] = keep2[tensor] + got2[tensor].astype(F32)
    for e in (1, 2, 3):
        to = lax.rem(tensor + e, N_T)
        scr[pl.ds(0, GROUP), :] = keep1[to] + got1[to].astype(F32)[:GROUP, :]
        sends1[e - 1][...] = scr[...].astype(BF16)
        sends2[e - 1][...] = (keep2[to] + got2[to].astype(F32)).astype(BF16)


def tensor_sum_kernel(own, r1, r2, r3, cen, send, cen_out, scr):
    total = own[...]
    center = cen[...]
    for r in (r1, r2, r3):
        v = r[...].astype(F32)
        total = total + v[:GROUP, :]
        center = center + v[GROUP : GROUP + 1, :] + v[GROUP + 1 : GROUP + 2, :]
    cen_out[...] = center
    high, low = split(center)
    scr[pl.ds(0, GROUP), :] = total
    scr[pl.ds(GROUP, 16), :] = rows_of(high, low, 16)
    send[...] = scr[...].astype(BF16)


def pair_sum_kernel(own, r1, r2, r3, pair, cen, total_out, send, cen_out, scr):
    v = pair[...].astype(F32)
    total = own[...] + v[:GROUP, :]
    for r in (r1, r2, r3):
        total = total + r[...].astype(F32)
    center = cen[...] + v[GROUP : GROUP + 1, :] + v[GROUP + 1 : GROUP + 2, :]
    total_out[...] = total
    cen_out[...] = center
    high, low = split(center)
    scr[pl.ds(0, GROUP), :] = total
    scr[pl.ds(GROUP, 16), :] = rows_of(high, low, 16)
    send[...] = scr[...].astype(BF16)


def grad_kernel(idx, own, r1, r2, r3, cen, root, gain, bias, x_ref, g_ref, cast, err):
    total = own[...]
    center = cen[...]
    for r in (r1, r2, r3):
        v = r[...].astype(F32)
        total = total + v[:GROUP, :]
        center = center + v[GROUP : GROUP + 1, :] + v[GROUP + 1 : GROUP + 2, :]
    center = center * (1.0 / D)
    x = x_ref[...].astype(F32)
    inv = 1.0 / root[...]
    grad_x = g_ref[...].astype(F32) + (total * gain[...] - x * inv * center) * inv
    cast[...] = grad_x.astype(BF16)
    start = (idx[2] // 2) * PIECE
    index = lax.broadcasted_iota(jnp.int32, (GROUP, TOK), 0)
    mine = (index >= start) & (index < start + PIECE)
    terms = jnp.where(mine, grad_x * (x - bias[...]), 0.0)
    err[...] = jnp.sum(terms, axis=0, keepdims=True)


def fetch_kernel(ids, decoder, _, dec, passed, sems):
    def each(act):
        for b in range(2):
            for r in range(CAP):
                index = ids[b, r]

                @pl.when(index >= 0)
                def _():
                    rows = pl.ds(pl.multiple_of(jnp.maximum(index, 0) * BLOCK, BLOCK), BLOCK)
                    into = dec.at[b, pl.ds(r * BLOCK, BLOCK)]
                    act(pltpu.make_async_copy(decoder.at[rows], into, sems.at[b, r]))

    each(lambda copy: copy.start())
    each(lambda copy: copy.wait())


def stack_kernel(a, b, c, out, sems):
    copies = [pltpu.make_async_copy(w, out.at[i], sems.at[i]) for i, w in enumerate((a, b, c))]
    for copy in copies:
        copy.start()
    for copy in copies:
        copy.wait()


def decode_kernel(idx, g0, g1, g2, g3, err, dec, own, s1, s2, s3, grad, scr, wide):
    place = 2 * lax.rem(idx[2], 2) + idx[3]
    flips = (place, 2 * (1 - lax.rem(idx[2], 2)) + idx[3], 2 * lax.rem(idx[2], 2) + 1 - idx[3])
    last = 2 * (1 - lax.rem(idx[2], 2)) + 1 - idx[3]
    for g, at in zip((g0, g1, g2, g3), flips + (last,)):
        rows = g[...].astype(F32)
        for k in range(N_Z // 2):
            start = pl.multiple_of((4 * k + at) * PIECE, 8)
            scr[pl.ds(start, PIECE), :] = rows[k * PIECE : (k + 1) * PIECE, :]
    grad[...] = scr[...].astype(BF16)
    tall = jnp.broadcast_to(err[...], (BLOCK, TOK)).T
    high, low = split(tall)
    lane = lax.broadcasted_iota(jnp.int32, (TOK, BLOCK), 1)
    wide[:, COLS:] = jnp.where(lane == 0, high, jnp.where(lane == 1, low, 0.0))
    for b in range(2):
        tokens = grad[:, b * BLOCK : (b + 1) * BLOCK]
        wide[b * BLOCK : (b + 1) * BLOCK, :COLS] = lax.dot_general(
            tokens, dec[b], (((0,), (1,)), ((), ())), preferred_element_type=F32
        )
    tensor = idx[1]
    own[...] = wide[pl.ds(pl.multiple_of(tensor * OWN_TOK, OWN_TOK), OWN_TOK), :]
    for e, out in ((1, s1), (2, s2), (3, s3)):
        to = lax.rem(tensor + e, N_T)
        rows = pl.ds(pl.multiple_of(to * OWN_TOK, OWN_TOK), OWN_TOK)
        out[...] = wide[rows, :].astype(BF16)


def product_sum_kernel(own, r1, r2, r3, out):
    total = own[...]
    for r in (r1, r2, r3):
        total = total + r[...].astype(F32)
    out[:, :COLS] = total[:, :COLS].astype(BF16)
    high, low = split(total[:, COLS : COLS + 1] + total[:, COLS + 1 : COLS + 2])
    lane = lax.broadcasted_iota(jnp.int32, (OWN_TOK, BLOCK), 1)
    out[:, COLS:] = jnp.where(lane == 0, high, jnp.where(lane == 1, low, 0.0)).astype(BF16)


def score_kernel(slots, got, acts, scores, err, scr):
    scr[...] = got[...].astype(F32)
    total = jnp.zeros((4, BLOCK), F32)
    for k in range(SLOTS):
        at = pl.ds(pl.multiple_of(slots[1, k] * BLOCK, BLOCK), BLOCK)
        value = scr[slots[0, k], :, at] * acts[:, k * BLOCK : (k + 1) * BLOCK].astype(F32)
        value = jnp.where(slots[2, k] > 0, value, 0.0)
        total += value
        scores[:, k * BLOCK : (k + 1) * BLOCK] = value.astype(BF16)
    extra = jnp.sum(scr[:, :, COLS:], axis=0)
    rest = jnp.concatenate([extra - total, jnp.zeros((4, BLOCK), F32)], axis=0).T
    err[...] = jnp.sum(rest, axis=0, keepdims=True)[:, :4] * (1.0 / math.sqrt(D))


def on_device(
    resid,
    out_grad,
    norm_gain,
    w_gate,
    w_up,
    w_down_t,
    decoder,
    dec_bias,
    block_ids,
    counts,
    latent_acts,
):
    dp, tensor, latent = (lax.axis_index(a) for a in ("dp", "tensor", "latent"))
    idx = jnp.stack([dp, tensor, latent // 2, latent % 2]).astype(jnp.int32)

    with jax.named_scope("slots"):
        owner = block_ids // SLOTS
        same = owner[:, :, None] == owner[:, None, :]
        before = jnp.tril(jnp.ones((SLOTS, SLOTS), bool), -1)
        rank = jnp.sum(same & before, axis=2, dtype=jnp.int32)
        live = jnp.arange(SLOTS, dtype=jnp.int32) < counts[:, None]
        mine = live & (owner == latent)
        takes = mine[:, :, None] & (rank[:, :, None] == jnp.arange(CAP))
        local = jnp.sum(jnp.where(takes, (block_ids % SLOTS)[:, :, None] + 1, 0), axis=1) - 1
        slots = jnp.stack([owner, rank, live.astype(jnp.int32)])[:, tensor // 2]
    with jax.named_scope("weight_rows"):
        rows = call(
            stack_kernel,
            "stack",
            [HBM] * 3,
            shape((3, HID, CHUNK), BF16),
            [pltpu.SemaphoreType.DMA((3,))],
            limit=60,
        )(w_gate.T, w_up.T, w_down_t.T)
        below = shift(rows, "dp", N_DP, 1)
        above = shift(rows, "dp", N_DP, -1)
        middle = HID // 2
        far_low = shift(below[:, :middle], "dp", N_DP, 1)
        far_high = shift(above[:, middle:], "dp", N_DP, -1)

    with jax.named_scope("token_features"):
        x_own, g_own = resid.T, out_grad.T
        column = lax.all_gather(jnp.concatenate([x_own, g_own]), "latent", axis=0)
        x_all = column[:, :PIECE].reshape(CHUNK, TOK)
        g_all = column[:, PIECE:].reshape(CHUNK, TOK)
        fetch = jnp.where(latent % 2 == 0, x_all, g_all)
        own = [shift(fetch, "tensor", N_T, e) for e in (1, 3, 2)]
        other = [swap_core(a) for a in own]

    with jax.named_scope("mlp"):
        row = shape((1, TOK), F32)
        early = call(
            early_kernel,
            "early",
            [SMEM] + [VMEM] * 6,
            (shape((D, TOK), BF16), shape((D, TOK), BF16), shape((8, TOK), F32)),
            limit=14,
        )(idx, x_all, g_all, own[0], own[1], other[0], other[1])
        keep1, keep2, send1, send2, cen, root = call(
            mlp_kernel,
            "mlp",
            [SMEM] + [VMEM] * 11,
            (
                shape((N_T, GROUP, TOK), F32),
                shape((N_T, GROUP, TOK), F32),
                shape((N_T, SENT, TOK), BF16),
                shape((N_T, GROUP, TOK), BF16),
                row,
                row,
            ),
            [
                pltpu.VMEM((D, TOK), BF16),
                pltpu.VMEM((D, TOK), BF16),
                pltpu.VMEM((2 * HID, TOK), BF16),
                pltpu.VMEM((CHUNK, TOK), F32),
                pltpu.VMEM((SENT, TOK), F32),
            ],
            limit=20,
        )(
            idx, *early, own[2], other[2], norm_gain.reshape(D // BLOCK, BLOCK),
            rows, below, above, far_low, far_high,
        )

    with jax.named_scope("hidden_sums"):
        tensor_shifts = (1, 2, 3)
        got1, got2 = swap_core(send1), swap_core(send2)
        group = shape((GROUP, TOK), F32)
        own1, own2, *sends, cen = call(
            core_sum_kernel,
            "core_sum",
            [SMEM] + [VMEM] * 5,
            (group, group)
            + (shape((SENT, TOK), BF16),) * 3
            + (shape((GROUP, TOK), BF16),) * 3
            + (row,),
            [pltpu.VMEM((SENT, TOK), F32)],
            limit=12,
        )(idx, keep1, keep2, got1, got2, cen)
        parts1 = [shift(s, "tensor", N_T, e) for e, s in zip(tensor_shifts, sends[:3])]
        parts2 = [shift(s, "tensor", N_T, e) for e, s in zip(tensor_shifts, sends[3:])]
        send, cen = call(
            tensor_sum_kernel,
            "tensor_sum",
            [VMEM] * 5,
            (shape((SENT, TOK), BF16), row),
            [pltpu.VMEM((SENT, TOK), F32)],
            limit=8,
        )(own1, *parts1, cen)
        pair = lax.ppermute(send, "latent", [(i, i ^ 2) for i in range(N_L)])
        total, send, cen = call(
            pair_sum_kernel,
            "pair_sum",
            [VMEM] * 6,
            (group, shape((SENT, TOK), BF16), row),
            [pltpu.VMEM((SENT, TOK), F32)],
            limit=8,
        )(own2, *parts2, pair, cen)
        got = [shift(send, "latent", N_L, 4 * d) for d in (1, 2, 3)]

        dec, total = pl.pallas_call(
            fetch_kernel,
            name="fetch",
            in_specs=[SMEM, HBM, ANY],
            out_specs=(VMEM, ANY),
            out_shape=(shape((2, COLS, CHUNK), BF16), group),
            input_output_aliases={2: 1},
            scratch_shapes=[pltpu.SemaphoreType.DMA((2, CAP))],
            compiler_params=pltpu.CompilerParams(vmem_limit_bytes=8 * 2**20),
        )(local.astype(jnp.int32), decoder, total)

        def group_rows(array):
            pieces = array.reshape(N_Z // 2, 4, PIECE, -1)
            return lax.dynamic_index_in_dim(pieces, latent % 4, 1, False).reshape(GROUP, -1)

        gain_own, bias_own = (
            group_rows(lax.dynamic_slice_in_dim(v, tensor * CHUNK, CHUNK, 0))
            for v in (norm_gain, dec_bias)
        )
        cast, err = call(
            grad_kernel,
            "grad",
            [SMEM] + [VMEM] * 10,
            (shape((GROUP, TOK), BF16), row),
            limit=8,
        )(idx, total, *got, cen, root, gain_own, bias_own, group_rows(x_all), group_rows(g_all))

    with jax.named_scope("decode"):
        across = lax.ppermute(cast, "latent", [(i, i ^ 2) for i in range(N_L)])
        kept, *sends = call(
            decode_kernel,
            "decode",
            [SMEM] + [VMEM] * 6,
            (shape((OWN_TOK, WIDE), F32),) + (shape((OWN_TOK, WIDE), BF16),) * 3,
            [
                pltpu.VMEM((CHUNK, TOK), BF16),
                pltpu.VMEM((CHUNK, TOK), F32),
                pltpu.VMEM((TOK, WIDE), F32),
            ],
            limit=14,
        )(idx, cast, across, swap_core(cast), swap_core(across), err, dec)

        moved = [shift(s, "tensor", N_T, e) for e, s in zip(tensor_shifts, sends)]
        products = call(
            product_sum_kernel, "product_sum", [VMEM] * 4, shape((OWN_TOK, WIDE), BF16), limit=8
        )(kept, *moved)

    with jax.named_scope("scores"):
        got = lax.all_to_all(products.reshape(N_L, 4, WIDE), "latent", 0, 0, tiled=True)
        scores, err = call(
            score_kernel,
            "score",
            [SMEM, VMEM, VMEM],
            (shape((4, SLOTS * BLOCK), BF16), shape((1, 4), F32)),
            [pltpu.VMEM((N_L, 4, WIDE), F32)],
            limit=8,
        )(slots, got, latent_acts)
    return scores, err.reshape(4)


def solution(mesh):
    return jax.shard_map(
        on_device,
        mesh=mesh,
        in_specs=(
            P("dp", ("tensor", "latent")),
            P("dp", ("tensor", "latent")),
            P(),
            P("dp", ("tensor", "latent")),
            P("dp", ("tensor", "latent")),
            P("dp", ("tensor", "latent")),
            P("latent", "tensor"),
            P(),
            P("dp", None),
            P("dp"),
            P(("dp", "tensor", "latent"), None),
        ),
        out_specs=(P(("dp", "tensor", "latent"), None), P(("dp", "tensor", "latent"))),
        check_vma=False,
    )
```
